32 devices in a mesh: pipe: 4 (over x, core), expert: 2 (over y), dp: 4 (over z).
Axes of the slice: x: 2, y: 2, z: 4, core: 2. Of those that a mesh axis runs over, the one named last changes fastest.
Arguments:
- inputs: bfloat16 [4, 1024, 4096], P('pipe', ('expert', 'dp')), may hold values from -6 to 6
- routes: int32 [4, 1024, 1], P('pipe', ('expert', 'dp')), may hold values from 0 to 1; in each aligned block of 128 rows (0 to 127, 128 to 255, ..., all dimensions but the last counted through in order) at most 80 rows name the same one
- router_scores: float32 [4, 1024, 8], P('pipe', ('expert', 'dp')), may hold values from -2 to 2
- cotangent: bfloat16 [4, 1024, 4096], P('pipe', ('expert', 'dp')), may hold values from -6 to 6
- w_gate: bfloat16 [4, 2, 768, 4096], P('pipe', 'expert', 'dp'), may hold values from -0.09375 to 0.09375
- w_up: bfloat16 [4, 2, 768, 4096], P('pipe', 'expert', 'dp'), may hold values from -0.09375 to 0.09375
- w_down: bfloat16 [4, 2, 768, 4096], P('pipe', 'expert', 'dp'), may hold values from -0.21875 to 0.21875
Outputs:
- score_grad: float32 [4, 1024, 8], P('pipe', ('expert', 'dp'))
- grad_prev: bfloat16 [4, 1024, 4096], P('pipe', ('expert', 'dp'))
- grad_gate: bfloat16 [4, 2, 768, 4096], P('pipe', 'expert', 'dp')
- grad_up: bfloat16 [4, 2, 768, 4096], P('pipe', 'expert', 'dp')
- grad_down: bfloat16 [4, 2, 768, 4096], P('pipe', 'expert', 'dp')
The draws below stay inside these ranges and needn't reach their ends.
Inputs may be any that keep to these rules, and one draw needn't show every extreme that they name: `routes`: among the 128 tokens of one device in one section (one block) no expert is named more than 80 times, and in every draw some block names some expert exactly 80 times. Every expert is named by some token.
All inputs are finite; a program needn't handle non-finite values.
Results may differ from the reference program's by a relative error of at most 0.02.
Values may be sent and summed in bfloat16 or wider, within the bound.
A program may use at most 128 MiB of HBM per device.

```python
import math
import jax
import jax.numpy as jnp
import numpy as np
from jax import lax

D = 4096
HIDDEN_SIZE = 768
CHOSEN = 8
TOK_DEV = 128
EXPERTS = 2
CAP = 80
BLOCKS = 8
TOKENS = 1024
HID_SLICE = 192
N_PIPE = 4
N_DP = 4


def level_of(own_key, dims, cuts, smallest, top_value):
    loudness, own = 1.0, jax.random.fold_in(own_key, 6)
    for dim, blocks in cuts:
        draws = jnp.exp(jax.random.uniform(jax.random.fold_in(own, dim), (blocks,), jnp.float32, smallest / len(cuts), top_value / len(cuts)))
        loudness = loudness * jnp.repeat(draws, dims[dim] // blocks).reshape([-1 if axis == dim else 1 for axis in range(len(dims))])
    return loudness


def assign_block(rng, own, number, rows, count, top, bound, slope):
    sequence = jax.random.permutation(rng, count)
    heavy_load, ordinary = portions_of(count, rows * top, bound, slope, True), portions_of(count, rows * top, bound, slope, False)
    places = jnp.arange(count)

    def named(tallies, rotation):
        used = int((tallies > 0).sum())
        fixed = max(1, used // 4)
        shifted = fixed + (places - fixed + rotation * (used - fixed)) % max(1, count - fixed)
        return jnp.zeros((count,), jnp.int32).at[sequence[jnp.where(places < fixed, places, shifted)]].set(jnp.asarray(tallies, jnp.int32))

    tallies = jnp.where(number % 4 == 0, named(heavy_load, number // 4), named(ordinary, number - number // 4 - 1))
    mixed = jax.random.permutation(jax.random.fold_in(own, 3), count)
    source_of, sink = mixed[0:count // 2 * 2:2], mixed[1:count // 2 * 2:2]
    room = jnp.minimum(tallies[source_of] - 1, bound - tallies[sink]) // 2
    room = jnp.where((source_of == sequence[0]) | (sink == sequence[0]) | (tallies[sink] == 0), 0, jnp.maximum(room, 0))
    shifted = jax.random.randint(jax.random.fold_in(own, 4), (count // 2,), 0, 1 << 20) % (room + 1)
    tallies = tallies.at[source_of].add(-shifted).at[sink].add(shifted)
    labels = jnp.searchsorted(jnp.cumsum(tallies), jnp.arange(rows * top), side="right").astype(jnp.int32)
    listing = labels.reshape(top, rows).T
    listing = listing[jax.random.permutation(jax.random.fold_in(own, 1), rows)]
    rotation = jax.random.randint(jax.random.fold_in(own, 2), (rows, 1), 0, top)
    return jnp.take_along_axis(listing, (jnp.arange(top)[None, :] + rotation) % top, axis=1)


def portions_of(amount, total, limit, slope, full):
    portions = [(1 << 20) // math.isqrt(grade ** slope) + 1 for grade in range(1, amount + 1)]
    largest = limit if full else min(limit, max(-(-total // amount), total * portions[0] // sum(portions)))
    least = 1 if total - largest >= amount - 1 else 0
    counts, surplus = [largest] + [least] * (amount - 1), total - largest - least * (amount - 1)
    while surplus > 0:
        candidates = [i for i in range(1, amount) if counts[i] < largest] or [i for i in range(1, amount) if counts[i] < limit]
        whole, remaining = sum([portions[i] for i in candidates]), surplus
        for i in candidates:
            addition = min(limit - counts[i], max(1, remaining * portions[i] // whole), surplus)
            counts[i] = counts[i] + addition
            surplus = surplus - addition
    return np.array(counts)


def bell_draw(own_key, extent, scale, reach, pieces=(), kind=jnp.bfloat16):
    values = jax.random.normal(own_key, extent, jnp.float32) * scale
    if len(pieces) > 0:
        values = level_of(own_key, extent, pieces, -0.22, 0.18) * values
    return jnp.clip(values, min=-reach, max=reach).astype(kind)


def setup_inputs(seed: int = 0) -> dict:
    splits = jax.random.split(jax.random.key(seed), 8)
    inputs = bell_draw(splits[0], (N_PIPE, TOKENS, D), 1.0, 6.0, ((0, 4), (1, 8)))
    routes_keys = jax.random.split(jax.random.fold_in(splits[1], 1), N_PIPE * TOKENS // TOK_DEV)
    routes_turns = jax.random.permutation(jax.random.fold_in(splits[1], 3), N_PIPE * TOKENS // TOK_DEV)
    routes = jax.vmap(lambda own, number: assign_block(jax.random.fold_in(splits[1], 2), own, number, TOK_DEV, EXPERTS, 1, CAP, 2))(routes_keys, routes_turns).reshape((N_PIPE, TOKENS, 1))
    router_scores = jnp.clip(jax.random.uniform(splits[2], (N_PIPE, TOKENS, CHOSEN), jnp.float32, -2.0, 2.0) * level_of(splits[2], (N_PIPE, TOKENS, CHOSEN), ((0, 4), (1, 8)), -0.4, 0.0), -2.0, 2.0)
    cotangent = bell_draw(splits[3], (N_PIPE, TOKENS, D), 1.0, 6.0, ((0, 4), (1, 8)))
    w_gate = bell_draw(splits[4], (N_PIPE, EXPERTS, HIDDEN_SIZE, D), D ** -0.5, 0.09375, ((0, 4), (1, 2), (2, 4)))
    w_up = bell_draw(splits[5], (N_PIPE, EXPERTS, HIDDEN_SIZE, D), D ** -0.5, 0.09375, ((0, 4), (1, 2), (2, 4)))
    w_down = bell_draw(splits[6], (N_PIPE, EXPERTS, HIDDEN_SIZE, D), HIDDEN_SIZE ** -0.5, 0.21875, ((0, 4), (1, 2), (2, 4)))
    return dict(inputs=inputs, routes=routes, router_scores=router_scores, cotangent=cotangent, w_gate=w_gate, w_up=w_up, w_down=w_down)


def block_tables(route_col, score_rows):
    expert_ids = jnp.arange(EXPERTS, dtype=jnp.int32)
    onehot = (route_col[:, None] == expert_ids).astype(jnp.int32)
    earlier = (jnp.cumsum(onehot, axis=0) - onehot).astype(jnp.int32)
    slot = jnp.sum(onehot * earlier, axis=1).astype(jnp.int32)
    position = (route_col * CAP + slot).astype(jnp.int32)
    raised = jnp.exp(score_rows)
    weights = raised / jnp.sum(raised, axis=1, keepdims=True)
    gate = lax.optimization_barrier(weights[:, 0].astype(jnp.bfloat16)).astype(jnp.float32)
    table = (position[:, None] == jnp.arange(EXPERTS * CAP, dtype=jnp.int32)).astype(jnp.float32)
    return weights, gate, table


def expert_pass(operands):
    rows_x, rows_grad, gate_mat, up_mat, down_mat = operands
    feature_contract = (((1,), (1,)), ((), ()))
    gate_pre = lax.dot_general(rows_x, gate_mat, feature_contract, preferred_element_type=jnp.float32)
    up_pre = lax.dot_general(rows_x, up_mat, feature_contract, preferred_element_type=jnp.float32)
    gate_sig = jax.nn.sigmoid(gate_pre)
    activated = (gate_pre * gate_sig * up_pre).astype(jnp.bfloat16)
    running = jnp.zeros((rows_x.shape[0], D), jnp.float32)
    for member in range(N_DP):
        start_col = member * HID_SLICE
        stop_col = start_col + HID_SLICE
        partial_value = jnp.dot(activated[:, start_col:stop_col], down_mat[start_col:stop_col], preferred_element_type=jnp.float32).astype(jnp.bfloat16)
        running = running + lax.optimization_barrier(partial_value).astype(jnp.float32)
    rows_y = running.astype(jnp.bfloat16)
    hidden_grad = lax.dot_general(rows_grad, down_mat, feature_contract, preferred_element_type=jnp.float32)
    pre_gate = (hidden_grad * up_pre * gate_sig * (1.0 + gate_pre * (1.0 - gate_sig))).astype(jnp.bfloat16)
    pre_up = (hidden_grad * gate_pre * gate_sig).astype(jnp.bfloat16)
    rows_contract = (((0,), (0,)), ((), ()))
    grad_down = lax.dot_general(activated, rows_grad, rows_contract, preferred_element_type=jnp.float32).astype(jnp.bfloat16)
    grad_gate = lax.dot_general(pre_gate, rows_x, rows_contract, preferred_element_type=jnp.float32).astype(jnp.bfloat16)
    grad_up = lax.dot_general(pre_up, rows_x, rows_contract, preferred_element_type=jnp.float32).astype(jnp.bfloat16)
    running = jnp.zeros((rows_x.shape[0], D), jnp.float32)
    for member in range(N_DP):
        start_col = member * HID_SLICE
        stop_col = start_col + HID_SLICE
        partial_value = jnp.dot(pre_gate[:, start_col:stop_col], gate_mat[start_col:stop_col], preferred_element_type=jnp.float32)
        partial_value = partial_value + jnp.dot(pre_up[:, start_col:stop_col], up_mat[start_col:stop_col], preferred_element_type=jnp.float32)
        running = running + lax.optimization_barrier(partial_value.astype(jnp.bfloat16)).astype(jnp.float32)
    rows_dx = running.astype(jnp.bfloat16)
    return rows_y, rows_dx, grad_gate, grad_up, grad_down


def section_pass(tokens_in, route_rows, score_rows, upstream, gate_all, up_all, down_all):
    route_b = route_rows[:, 0].reshape(BLOCKS, TOK_DEV)
    score_b = score_rows.reshape(BLOCKS, TOK_DEV, CHOSEN)
    weights, gate, table = jax.vmap(block_tables)(route_b, score_b)
    tokens_b = tokens_in.reshape(BLOCKS, TOK_DEV, D).astype(jnp.float32)
    upstream_b = upstream.reshape(BLOCKS, TOK_DEV, D).astype(jnp.float32)

    def to_rows(values):
        return values.reshape(BLOCKS, EXPERTS, CAP, D).transpose(1, 0, 2, 3).reshape(EXPERTS, BLOCKS * CAP, D)

    def to_blocks(values):
        return values.reshape(EXPERTS, BLOCKS, CAP, D).transpose(1, 0, 2, 3).reshape(BLOCKS, EXPERTS * CAP, D).astype(jnp.float32)

    rows_x = to_rows(jnp.einsum('btp,btk->bpk', table, tokens_b)).astype(jnp.bfloat16)
    scaled = lax.optimization_barrier((gate[:, :, None] * upstream_b).astype(jnp.bfloat16)).astype(jnp.float32)
    rows_grad = to_rows(jnp.einsum('btp,btk->bpk', table, scaled)).astype(jnp.bfloat16)
    rows_y, rows_dx, grad_gate, grad_up, grad_down = lax.map(expert_pass, (rows_x, rows_grad, gate_all, up_all, down_all))
    blocks_y = to_blocks(rows_y)
    scores_grad = jnp.einsum('btk,bpk->btp', upstream_b, blocks_y)
    gate_grad = jnp.sum(table * scores_grad, axis=2)
    is_first = (jnp.arange(CHOSEN) == 0).astype(jnp.float32)
    score_grad = gate_grad[:, :, None] * weights[:, :, 0:1] * (is_first - weights)
    input_grad = jnp.einsum('btp,bpk->btk', table, to_blocks(rows_dx)).astype(jnp.bfloat16).reshape(TOKENS, D)
    return score_grad.reshape(TOKENS, CHOSEN), input_grad, grad_gate, grad_up, grad_down


def reference(inputs, routes, router_scores, cotangent, w_gate, w_up, w_down):
    results = []
    for section_id in range(N_PIPE):
        results.append(section_pass(inputs[section_id], routes[section_id], router_scores[section_id], cotangent[section_id], w_gate[section_id], w_up[section_id], w_down[section_id]))
    score_grad = jnp.stack([item[0] for item in results])
    handed = [item[1] for item in results[1:]] + [jnp.zeros((TOKENS, D), jnp.bfloat16)]
    grad_prev = jnp.stack(handed)
    grad_gate = jnp.stack([item[2] for item in results])
    grad_up = jnp.stack([item[3] for item in results])
    grad_down = jnp.stack([item[4] for item in results])
    return (score_grad, grad_prev, grad_gate, grad_up, grad_down)
```

```python
import functools

import jax
import jax.numpy as jnp
from jax import lax
from jax.experimental import pallas as pl
from jax.experimental.pallas import tpu as pltpu
from jax.sharding import PartitionSpec as P

MESH = pl.DeviceIdType.MESH
NT = (((1,), (1,)), ((), ()))
TN = (((0,), (0,)), ((), ()))


def compute_order(k, n):
    order = [k]
    for d in range(1, n):
        order += [b for b in (k - d, k + d) if 0 <= b < n]
    if n > 2 and k in (0, n - 1):
        order = [k] + order[2:] + [order[1]]
    if k >= n // 2 and 0 < k < n - 1:
        order = [k]
        for d in range(1, n):
            order += [b for b in (k + d, k - d) if 0 <= b < n]
    return order


def finish_order(k, n):
    if k in (0, n - 1):
        return []
    rightward = list(range(k + 1, n))
    leftward = list(range(k - 1, -1, -1))
    return rightward + leftward if k < n // 2 else leftward + rightward


def kernel(
    dims, x_ref, up_ref, gate_ref, tab_ref, nxt_ref, wg_ref, wu_ref, wd_ref,
    out_ref, gg_ref, gu_ref, gd_ref, s_ref,
    stage, xb, yb, dxb, dxr, hrecv, act, pg, pu, sbuf, srecv,
    ey_send, ey_recv, f_send, f_recv, r_send, r_recv, s_send, s_recv, h_send, h_recv,
):
    pipes, experts, n, cap, depth = dims
    rows = experts * cap
    p, y, z = lax.axis_index("pipe"), lax.axis_index("expert"), lax.axis_index("dp")
    tokens, width = x_ref.shape

    def peer(de, dz):
        return lax.rem(y + de, experts), lax.rem(z + dz, n)

    others = [(de, dz) for de in range(experts) for dz in range(n) if (de, dz) != (0, 0)]

    barrier = pltpu.get_barrier_semaphore()
    for de, dz in others:
        ey, ez = peer(de, dz)
        pl.semaphore_signal(barrier, inc=1, device_id=(p, ey, ez), device_id_type=MESH)

    @pl.when(p > 0)
    def _():
        for e in range(experts):
            pl.semaphore_signal(barrier, inc=1, device_id=(p - 1, e, z), device_id_type=MESH)

    @pl.when(p < pipes - 1)
    def _():
        for e in range(experts):
            pl.semaphore_signal(barrier, inc=1, device_id=(p + 1, e, z), device_id_type=MESH)

    def block(ref, b):
        return ref.at[pl.ds(b * rows, rows)]

    tab = tab_ref[...]
    step = min(512, width)

    def pack(t, buffer):
        def tile(j, c):
            cols = pl.ds(pl.multiple_of(j * step, step), step)
            if t == 0:
                vals = x_ref[:, cols]
            else:
                vals = (gate_ref[...] * up_ref[:, cols].astype(jnp.float32)).astype(jnp.bfloat16)
            stage[t, :, cols] = jnp.dot(tab, vals, preferred_element_type=jnp.float32).astype(jnp.bfloat16)
            return c

        lax.fori_loop(0, width // step, tile, 0)

    def exchange(t, buffer, de):
        e = lax.rem(y + de, experts)
        return pltpu.make_async_remote_copy(
            src_ref=stage.at[t, pl.ds(pl.multiple_of(e * cap, 16), cap)],
            dst_ref=buffer.at[pl.ds(pl.multiple_of(z * rows + y * cap, 16), cap)],
            send_sem=ey_send.at[t, de], recv_sem=ey_recv.at[t, de],
            device_id=(p, e, z), device_id_type=MESH,
        )

    pack(0, xb)
    around = (p > 0).astype(jnp.int32) + (p < pipes - 1).astype(jnp.int32)
    pl.semaphore_wait(barrier, len(others) + experts * around)

    for t, buffer in ((0, xb), (1, yb)):
        if t:
            pack(1, yb)
        for de in range(1, experts):
            exchange(t, buffer, de).start()
        own = pl.ds(pl.multiple_of(z * rows + y * cap, 16), cap)
        buffer[own] = stage[t, pl.ds(pl.multiple_of(y * cap, 16), cap)]

    def forward(b, t, side):
        buffer = (xb, yb)[t]
        return pltpu.make_async_remote_copy(
            src_ref=block(buffer, b), dst_ref=block(buffer, b),
            send_sem=f_send.at[side, b, t], recv_sem=f_recv.at[side, b, t],
            device_id=(p, y, z + (1 if side else -1)), device_id_type=MESH,
        )

    def running(k, b, side):
        slot = n if (not side and b == k - 1) else b
        return pltpu.make_async_remote_copy(
            src_ref=block(dxb, b), dst_ref=block(dxr, slot),
            send_sem=r_send.at[b], recv_sem=r_recv.at[slot],
            device_id=(p, y, z + (1 if side else -1)), device_id_type=MESH,
        )

    def taken(slot):
        pltpu.make_async_copy(block(dxr, slot), block(dxr, slot), r_recv.at[slot]).wait()

    def arrive(k, b, t):
        side = 1 if b < k else 0
        forward(b, t, side).wait_recv()
        if side and k < n - 1 or not side and k > 0:
            forward(b, t, side).start()

    def near_end(k, side):
        return n > 2 and (side and k == n - 2 or not side and k == 1)

    def sides(k):
        return ([1] if k < n - 1 else []) + ([0] if k > 0 else [])

    for t, buffer in ((0, xb), (1, yb)):
        for de in range(1, experts):
            exchange(t, buffer, de).wait_recv()
        for k in range(n):
            @pl.when(z == k)
            def _():
                for side in sides(k):
                    if t == 0 or not near_end(k, side):
                        forward(k, t, side).start()

    def work(b):
        off = pl.multiple_of(b * rows, 16)
        here = pl.ds(off, rows)
        deep = min(1024, width)

        def into(j, c):
            cols = pl.ds(pl.multiple_of(j * deep, deep), deep)
            xt, yt = xb[here, cols], yb[here, cols]
            g, u, a = c
            g = g + lax.dot_general(xt, wg_ref[:, cols], NT, preferred_element_type=jnp.float32)
            u = u + lax.dot_general(xt, wu_ref[:, cols], NT, preferred_element_type=jnp.float32)
            a = a + lax.dot_general(yt, wd_ref[:, cols], NT, preferred_element_type=jnp.float32)
            return g, u, a

        zero = jnp.zeros((rows, depth), jnp.float32)
        g, u, a = lax.fori_loop(0, width // deep, into, (zero, zero, zero))
        sig = 1.0 / (1.0 + jnp.exp(-g))
        silu = g * sig
        hidden = (silu * u).astype(jnp.bfloat16)
        act[here] = hidden
        total = jnp.sum(hidden.astype(jnp.float32) * a, axis=1, keepdims=True)
        sbuf[here] = jnp.broadcast_to(total, (rows, 128))
        dg = (a * u * sig * (1.0 + g * (1.0 - sig))).astype(jnp.bfloat16)
        du = (a * silu).astype(jnp.bfloat16)
        pg[here] = dg
        pu[here] = du

        def back(j, c):
            cols = pl.ds(pl.multiple_of(j * step, step), step)
            part = jnp.dot(pg[here], wg_ref[:, cols], preferred_element_type=jnp.float32)
            part = part + jnp.dot(pu[here], wu_ref[:, cols], preferred_element_type=jnp.float32)
            dxb[here, cols] = part.astype(jnp.bfloat16)
            return c

        lax.fori_loop(0, width // step, back, 0)

    orders = [compute_order(k, n) for k in range(n)]
    for i in range(n):
        if i:
            for k in range(n):
                @pl.when(z == k)
                def _():
                    b = orders[k][i]
                    if n > 2 and k in (0, n - 1):
                        if i == 1:
                            arrive(k, orders[k][n - 1], 0)
                        for t in range(2):
                            if t or i < n - 1:
                                arrive(k, b, t)
                    else:
                        d = abs(b - k)
                        pair = [c for c in (k - d, k + d) if 0 <= c < n]
                        if all(orders[k].index(c) >= i for c in pair):
                            for t in range(2):
                                for c in pair:
                                    arrive(k, c, t)
                        if i == n - 1:
                            for side in sides(k):
                                if near_end(k, side):
                                    forward(k, 1, side).start()
        b = 0
        for k in range(n):
            b = b + (z == k).astype(jnp.int32) * orders[k][i]
        work(b)
        if i:
            for k in (0, n - 1):
                @pl.when(z == k)
                def _():
                    running(k, orders[k][i], 0 if k else 1).start()

    def tell(de, dz):
        ey, ez = peer(de, dz)
        return pltpu.make_async_remote_copy(
            src_ref=sbuf.at[pl.ds(pl.multiple_of(ez * rows + ey * cap, 16), cap)],
            dst_ref=srecv.at[z, pl.ds(pl.multiple_of(y * cap, 16), cap)],
            send_sem=s_send.at[de, dz], recv_sem=s_recv.at[de, dz],
            device_id=(p, ey, ez), device_id_type=MESH,
        )

    for de, dz in others:
        tell(de, dz).start()
    srecv[z, pl.ds(pl.multiple_of(y * cap, 16), cap)] = sbuf[
        pl.ds(pl.multiple_of(z * rows + y * cap, 16), cap)
    ]

    def weights(j, c):
        cols = pl.ds(pl.multiple_of(j * step, step), step)
        yt, xt = yb[:, cols], xb[:, cols]
        gd_ref[:, cols] = lax.dot_general(act[...], yt, TN, preferred_element_type=jnp.float32).astype(jnp.bfloat16)
        gg_ref[:, cols] = lax.dot_general(pg[...], xt, TN, preferred_element_type=jnp.float32).astype(jnp.bfloat16)
        gu_ref[:, cols] = lax.dot_general(pu[...], xt, TN, preferred_element_type=jnp.float32).astype(jnp.bfloat16)
        return c

    lax.fori_loop(0, width // step, weights, 0)

    def add(b, slots):
        def some(j, c):
            here = pl.ds(pl.multiple_of(b * rows + j * 16, 16), 16)
            total = dxb[here].astype(jnp.float32)
            for slot in slots:
                total = total + dxr[pl.ds(pl.multiple_of(slot * rows + j * 16, 16), 16)].astype(jnp.float32)
            dxb[here] = total.astype(jnp.bfloat16)
            return c

        lax.fori_loop(0, rows // 16, some, 0)

    for k in range(n):
        @pl.when(z == k)
        def _():
            for b in finish_order(k, n):
                side = 1 if b > k else 0
                taken(b)
                add(b, [b])
                running(k, b, side).start()
            slots = ([k] if k > 0 else []) + ([n] if k < n - 1 else [])
            for slot in slots:
                taken(slot)
            add(k, slots)

    def hand(e):
        return pltpu.make_async_remote_copy(
            src_ref=dxb.at[pl.ds(pl.multiple_of(z * rows + e * cap, 16), cap)],
            dst_ref=hrecv.at[pl.ds(pl.multiple_of(y * cap, 16), cap)],
            send_sem=h_send.at[e], recv_sem=h_recv.at[y],
            device_id=(p - 1, e, z), device_id_type=MESH,
        )

    @pl.when(p > 0)
    def _():
        for e in range(experts):
            hand(e).start()

    for de, dz in others:
        tell(de, dz).wait_recv()
    total = srecv[0]
    for k in range(1, n):
        total = total + srecv[k]
    s_ref[...] = total

    @pl.when(p < pipes - 1)
    def _():
        for e in range(experts):
            pltpu.make_async_copy(hrecv.at[pl.ds(e * cap, cap)], hrecv.at[pl.ds(e * cap, cap)], h_recv.at[e]).wait()

        def tile(j, c):
            cols = pl.ds(pl.multiple_of(j * step, step), step)
            out_ref[:, cols] = lax.dot_general(
                nxt_ref[...], hrecv[:, cols], TN, preferred_element_type=jnp.float32
            ).astype(jnp.bfloat16)
            return c

        lax.fori_loop(0, width // step, tile, 0)

    @pl.when(p == pipes - 1)
    def _():
        out_ref[...] = jnp.zeros_like(out_ref)

    for t, buffer in ((0, xb), (1, yb)):
        for de in range(1, experts):
            exchange(t, buffer, de).wait_send()
    for de, dz in others:
        tell(de, dz).wait_send()
    for k in range(n):
        @pl.when(z == k)
        def _():
            for b in range(n):
                for side in sides(k):
                    if b == k or (b < k and side) or (b > k and not side):
                        for t in range(2):
                            forward(b, t, side).wait_send()
                if b != k:
                    running(k, b, 1 if b > k else 0).wait_send()

    @pl.when(p > 0)
    def _():
        for e in range(experts):
            hand(e).wait_send()


def tables(route_col, experts, capacity, padded):
    expert_ids = jnp.arange(experts, dtype=jnp.int32)
    onehot = (route_col[:, None] == expert_ids).astype(jnp.int32)
    earlier = jnp.cumsum(onehot, axis=0) - onehot
    slot = jnp.sum(onehot * earlier, axis=1)
    position = route_col * padded + slot
    return (jnp.arange(experts * padded, dtype=jnp.int32)[:, None] == position[None, :])


def per_device(inputs, routes, router_scores, cotangent, w_gate, w_up, w_down):
    experts, n, pipes = lax.axis_size("expert"), lax.axis_size("dp"), lax.axis_size("pipe")
    tokens, width = inputs.shape[1:]
    depth = w_gate.shape[2]
    capacity = max(2, tokens * 5 // (4 * experts))
    cap = -(-capacity // 16) * 16
    rows = experts * cap
    route_col = routes[0, :, 0]
    behind = lax.ppermute(route_col, "pipe", [(i + 1, i) for i in range(pipes - 1)])
    table = tables(route_col, experts, capacity, cap)
    following = tables(behind, experts, capacity, cap).astype(jnp.bfloat16)
    raised = jnp.exp(router_scores[0])
    weights = raised / jnp.sum(raised, axis=1, keepdims=True)
    gate = lax.optimization_barrier(weights[:, 0:1].astype(jnp.bfloat16)).astype(jnp.float32)

    vmem = pl.BlockSpec(memory_space=pltpu.VMEM)
    half, full = jnp.bfloat16, jnp.float32
    dma = pltpu.SemaphoreType.DMA
    grad = jax.ShapeDtypeStruct((depth, width), half)
    handed, grad_gate, grad_up, grad_down, sums = pl.pallas_call(
        functools.partial(kernel, (pipes, experts, n, cap, depth)),
        out_shape=(
            jax.ShapeDtypeStruct((tokens, width), half), grad, grad, grad,
            jax.ShapeDtypeStruct((rows, 128), full),
        ),
        in_specs=[vmem] * 8,
        out_specs=(vmem,) * 5,
        scratch_shapes=[
            pltpu.VMEM((2, rows, width), half),
            pltpu.VMEM((n * rows, width), half),
            pltpu.VMEM((n * rows, width), half),
            pltpu.VMEM((n * rows, width), half),
            pltpu.VMEM(((n + 1) * rows, width), half),
            pltpu.VMEM((rows, width), half),
            pltpu.VMEM((n * rows, depth), half),
            pltpu.VMEM((n * rows, depth), half),
            pltpu.VMEM((n * rows, depth), half),
            pltpu.VMEM((n * rows, 128), full),
            pltpu.VMEM((n, rows, 128), full),
            dma((2, experts)), dma((2, experts)),
            dma((2, n, 2)), dma((2, n, 2)),
            dma((n,)), dma((n + 1,)),
            dma((experts, n)), dma((experts, n)),
            dma((experts,)), dma((experts,)),
        ],
        compiler_params=pltpu.CompilerParams(
            collective_id=0, has_side_effects=True, vmem_limit_bytes=62 * 1024 * 1024
        ),
    )(
        inputs[0], cotangent[0], gate, table.astype(half), following,
        w_gate[0, 0], w_up[0, 0], w_down[0, 0],
    )
    gate_grad = jnp.sum(jnp.where(table, sums[:, 0:1], 0.0), axis=0)[:, None] / gate
    is_first = (jnp.arange(router_scores.shape[2]) == 0).astype(full)
    score_grad = gate_grad * weights[:, 0:1] * (is_first - weights)
    return (
        score_grad[None],
        handed[None],
        grad_gate[None, None],
        grad_up[None, None],
        grad_down[None, None],
    )


def solution(mesh):
    rows = P("pipe", ("expert", "dp"), None)
    mats = P("pipe", "expert", "dp", None)
    return jax.shard_map(
        per_device, mesh=mesh, in_specs=(rows,) * 4 + (mats,) * 3,
        out_specs=(rows, rows, mats, mats, mats), check_vma=False,
    )
```

```python
import functools

import jax
import jax.numpy as jnp
from jax import lax
from jax.experimental import pallas as pl
from jax.experimental.pallas import tpu as pltpu
from jax.sharding import PartitionSpec as P

MESH = pl.DeviceIdType.MESH
NT = (((1,), (1,)), ((), ()))
TN = (((0,), (0,)), ((), ()))


def compute_order(k, n):
    order = [k]
    for d in range(1, n):
        order += [b for b in (k - d, k + d) if 0 <= b < n]
    if n > 2 and k in (0, n - 1):
        order = [k] + order[2:] + [order[1]]
    if k >= n // 2 and 0 < k < n - 1:
        order = [k]
        for d in range(1, n):
            order += [b for b in (k + d, k - d) if 0 <= b < n]
    return order


def finish_order(k, n):
    if k in (0, n - 1):
        return []
    rightward = list(range(k + 1, n))
    leftward = list(range(k - 1, -1, -1))
    return rightward + leftward if k < n // 2 else leftward + rightward


def kernel(
    dims, x_ref, up_ref, gate_ref, tab_ref, nxt_ref, wg_ref, wu_ref, wd_ref,
    out_ref, gg_ref, gu_ref, gd_ref, s_ref,
    stage, xb, yb, dxb, dxr, hrecv, act, pg, pu, sbuf, srecv,
    ey_send, ey_recv, f_send, f_recv, r_send, r_recv, s_send, s_recv, h_send, h_recv,
):
    pipes, experts, n, cap, depth = dims
    rows = experts * cap
    p, y, z = lax.axis_index("pipe"), lax.axis_index("expert"), lax.axis_index("dp")
    tokens, width = x_ref.shape

    def peer(de, dz):
        return lax.rem(y + de, experts), lax.rem(z + dz, n)

    others = [(de, dz) for de in range(experts) for dz in range(n) if (de, dz) != (0, 0)]

    barrier = pltpu.get_barrier_semaphore()
    for de, dz in others:
        ey, ez = peer(de, dz)
        pl.semaphore_signal(barrier, inc=1, device_id=(p, ey, ez), device_id_type=MESH)

    @pl.when(p > 0)
    def _():
        for e in range(experts):
            pl.semaphore_signal(barrier, inc=1, device_id=(p - 1, e, z), device_id_type=MESH)

    @pl.when(p < pipes - 1)
    def _():
        for e in range(experts):
            pl.semaphore_signal(barrier, inc=1, device_id=(p + 1, e, z), device_id_type=MESH)

    begin, length = (0, cap), (cap, rows - cap)

    def piece(ref, b, q):
        return ref.at[pl.ds(pl.multiple_of(b * rows + begin[q], 16), length[q])]

    tab = tab_ref[...]
    step = min(512, width)

    def pack(t, buffer):
        def tile(j, c):
            cols = pl.ds(pl.multiple_of(j * step, step), step)
            if t == 0:
                vals = x_ref[:, cols]
            else:
                vals = (gate_ref[...] * up_ref[:, cols].astype(jnp.float32)).astype(jnp.bfloat16)
            stage[t, :, cols] = jnp.dot(tab, vals, preferred_element_type=jnp.float32).astype(jnp.bfloat16)
            return c

        lax.fori_loop(0, width // step, tile, 0)

    def exchange(t, buffer, de):
        e = lax.rem(y + de, experts)
        return pltpu.make_async_remote_copy(
            src_ref=stage.at[t, pl.ds(pl.multiple_of(e * cap, 16), cap)],
            dst_ref=buffer.at[pl.ds(pl.multiple_of(z * rows + (experts - de) * cap, 16), cap)],
            send_sem=ey_send.at[t, de], recv_sem=ey_recv.at[t, de],
            device_id=(p, e, z), device_id_type=MESH,
        )

    pack(0, xb)
    around = (p > 0).astype(jnp.int32) + (p < pipes - 1).astype(jnp.int32)
    pl.semaphore_wait(barrier, len(others) + experts * around)

    def forward(b, t, q, side):
        buffer = (xb, yb)[t]
        return pltpu.make_async_remote_copy(
            src_ref=piece(buffer, b, q), dst_ref=piece(buffer, b, q),
            send_sem=f_send.at[side, b, t, q], recv_sem=f_recv.at[side, b, t, q],
            device_id=(p, y, z + (1 if side else -1)), device_id_type=MESH,
        )

    def running(k, b, q, side):
        slot = n if (not side and b == k - 1) else b
        return pltpu.make_async_remote_copy(
            src_ref=piece(dxb, b, q), dst_ref=piece(dxr, slot, q),
            send_sem=r_send.at[b, q], recv_sem=r_recv.at[slot, q],
            device_id=(p, y, z + (1 if side else -1)), device_id_type=MESH,
        )

    def taken(slot, q):
        whole = piece(dxr, slot, q)
        pltpu.make_async_copy(whole, whole, r_recv.at[slot, q]).wait()

    def arrive(k, b, t, q):
        side = 1 if b < k else 0
        forward(b, t, q, side).wait_recv()
        if side and k < n - 1 or not side and k > 0:
            forward(b, t, q, side).start()

    def near_end(k, side):
        return n > 2 and (side and k == n - 2 or not side and k == 1)

    def sides(k):
        return ([1] if k < n - 1 else []) + ([0] if k > 0 else [])

    def depart(t, q):
        for k in range(n):
            @pl.when(z == k)
            def _():
                for side in sides(k):
                    if t == 0 or not near_end(k, side):
                        forward(k, t, q, side).start()

    for t, buffer in ((0, xb), (1, yb)):
        if t:
            pack(1, yb)
        for de in range(1, experts):
            exchange(t, buffer, de).start()
        buffer[pl.ds(pl.multiple_of(z * rows, 16), cap)] = stage[t, pl.ds(pl.multiple_of(y * cap, 16), cap)]
        depart(t, 0)
    for t, buffer in ((0, xb), (1, yb)):
        for de in range(1, experts):
            exchange(t, buffer, de).wait_recv()
        depart(t, 1)

    def work(b, start, size):
        off = pl.multiple_of(b * rows + start, 16)
        here = pl.ds(off, size)
        deep = min(1024, width)

        def into(j, c):
            cols = pl.ds(pl.multiple_of(j * deep, deep), deep)
            xt, yt = xb[here, cols], yb[here, cols]
            g, u, a = c
            g = g + lax.dot_general(xt, wg_ref[:, cols], NT, preferred_element_type=jnp.float32)
            u = u + lax.dot_general(xt, wu_ref[:, cols], NT, preferred_element_type=jnp.float32)
            a = a + lax.dot_general(yt, wd_ref[:, cols], NT, preferred_element_type=jnp.float32)
            return g, u, a

        zero = jnp.zeros((size, depth), jnp.float32)
        g, u, a = lax.fori_loop(0, width // deep, into, (zero, zero, zero))
        sig = 1.0 / (1.0 + jnp.exp(-g))
        silu = g * sig
        hidden = (silu * u).astype(jnp.bfloat16)
        act[here] = hidden
        total = jnp.sum(hidden.astype(jnp.float32) * a, axis=1, keepdims=True)
        sbuf[here] = jnp.broadcast_to(total, (size, 128))
        dg = (a * u * sig * (1.0 + g * (1.0 - sig))).astype(jnp.bfloat16)
        du = (a * silu).astype(jnp.bfloat16)
        pg[here] = dg
        pu[here] = du

        def back(j, c):
            cols = pl.ds(pl.multiple_of(j * step, step), step)
            part = jnp.dot(pg[here], wg_ref[:, cols], preferred_element_type=jnp.float32)
            part = part + jnp.dot(pu[here], wu_ref[:, cols], preferred_element_type=jnp.float32)
            dxb[here, cols] = part.astype(jnp.bfloat16)
            return c

        lax.fori_loop(0, width // step, back, 0)

    orders = [compute_order(k, n) for k in range(n)]
    both = ((0, 0), (1, 0), (0, 1), (1, 1))
    for i in range(n):
        b = 0
        for k in range(n):
            b = b + (z == k).astype(jnp.int32) * orders[k][i]
        last = n > 1 and i == n - 1
        for part in ((0, 1) if last else (None,)):
            items = [item for item in both if part is None or item[1] == part]
            for k in range(n) if i else ():
                @pl.when(z == k)
                def _():
                    c = orders[k][i]
                    if k in (0, n - 1):
                        for t, q in items:
                            arrive(k, c, t, q)
                    else:
                        d = abs(c - k)
                        pair = [e for e in (k - d, k + d) if 0 <= e < n]
                        if last and len(pair) == 1 or not last and all(orders[k].index(e) >= i for e in pair):
                            for t, q in items:
                                for e in pair:
                                    arrive(k, e, t, q)
                        if last and part == 1:
                            for side in sides(k):
                                if near_end(k, side):
                                    forward(k, 1, 0, side).start()
            if part is None:
                work(b, 0, rows)
            else:
                work(b, begin[part], length[part])
            if last and part == 1:
                for k in range(n):
                    for side in sides(k):
                        if near_end(k, side):
                            @pl.when(z == k)
                            def _():
                                forward(k, 1, 1, side).start()
            if i:
                for k in (0, n - 1):
                    @pl.when((z == k) & (p > 0))
                    def _():
                        for q in (0, 1) if part is None else (part,):
                            running(k, orders[k][i], q, 0 if k else 1).start()

    def tell(de, dz):
        ey, ez = peer(de, dz)
        return pltpu.make_async_remote_copy(
            src_ref=sbuf.at[pl.ds(pl.multiple_of(ez * rows + de * cap, 16), cap)],
            dst_ref=srecv.at[z, pl.ds(pl.multiple_of(y * cap, 16), cap)],
            send_sem=s_send.at[de, dz], recv_sem=s_recv.at[de, dz],
            device_id=(p, ey, ez), device_id_type=MESH,
        )

    for de, dz in others:
        tell(de, dz).start()
    srecv[z, pl.ds(pl.multiple_of(y * cap, 16), cap)] = sbuf[
        pl.ds(pl.multiple_of(z * rows, 16), cap)
    ]

    def weights(j, c):
        cols = pl.ds(pl.multiple_of(j * step, step), step)
        yt, xt = yb[:, cols], xb[:, cols]
        gd_ref[:, cols] = lax.dot_general(act[...], yt, TN, preferred_element_type=jnp.float32).astype(jnp.bfloat16)
        gg_ref[:, cols] = lax.dot_general(pg[...], xt, TN, preferred_element_type=jnp.float32).astype(jnp.bfloat16)
        gu_ref[:, cols] = lax.dot_general(pu[...], xt, TN, preferred_element_type=jnp.float32).astype(jnp.bfloat16)
        return c

    lax.fori_loop(0, width // step, weights, 0)

    def add(b, slots, q):
        def some(j, c):
            here = pl.ds(pl.multiple_of(b * rows + begin[q] + j * 16, 16), 16)
            total = dxb[here].astype(jnp.float32)
            for slot in slots:
                there = pl.ds(pl.multiple_of(slot * rows + begin[q] + j * 16, 16), 16)
                total = total + dxr[there].astype(jnp.float32)
            dxb[here] = total.astype(jnp.bfloat16)
            return c

        lax.fori_loop(0, length[q] // 16, some, 0)

    def hand(de):
        return pltpu.make_async_remote_copy(
            src_ref=dxb.at[pl.ds(pl.multiple_of(z * rows + de * cap, 16), cap)],
            dst_ref=hrecv.at[pl.ds(pl.multiple_of(y * cap, 16), cap)],
            send_sem=h_send.at[de], recv_sem=h_recv.at[y],
            device_id=(p - 1, lax.rem(y + de, experts), z), device_id_type=MESH,
        )

    for k in range(n):
        @pl.when((z == k) & (p > 0))
        def _():
            for b in finish_order(k, n):
                for q in (0, 1):
                    taken(b, q)
                    add(b, [b], q)
                    running(k, b, q, 1 if b > k else 0).start()
            slots = ([k] if k > 0 else []) + ([n] if k < n - 1 else [])
            for q in (0, 1):
                for slot in slots:
                    taken(slot, q)
                add(k, slots, q)
                for de in (range(1, experts) if q else (0,)):
                    hand(de).start()

    for de, dz in others:
        tell(de, dz).wait_recv()
    total = srecv[0]
    for k in range(1, n):
        total = total + srecv[k]
    s_ref[...] = total

    @pl.when(p < pipes - 1)
    def _():
        for e in range(experts):
            pltpu.make_async_copy(hrecv.at[pl.ds(e * cap, cap)], hrecv.at[pl.ds(e * cap, cap)], h_recv.at[e]).wait()

        def tile(j, c):
            cols = pl.ds(pl.multiple_of(j * step, step), step)
            out_ref[:, cols] = lax.dot_general(
                nxt_ref[...], hrecv[:, cols], TN, preferred_element_type=jnp.float32
            ).astype(jnp.bfloat16)
            return c

        lax.fori_loop(0, width // step, tile, 0)

    @pl.when(p == pipes - 1)
    def _():
        out_ref[...] = jnp.zeros_like(out_ref)

    for t, buffer in ((0, xb), (1, yb)):
        for de in range(1, experts):
            exchange(t, buffer, de).wait_send()
    for de, dz in others:
        tell(de, dz).wait_send()
    for k in range(n):
        @pl.when(z == k)
        def _():
            for b in range(n):
                for side in sides(k):
                    if b == k or (b < k and side) or (b > k and not side):
                        for t, q in both:
                            forward(b, t, q, side).wait_send()

        @pl.when((z == k) & (p > 0))
        def _():
            for b in range(n):
                if b != k:
                    for q in (0, 1):
                        running(k, b, q, 1 if b > k else 0).wait_send()

    @pl.when(p > 0)
    def _():
        for de in range(experts):
            hand(de).wait_send()


def tables(route_col, experts, capacity, padded):
    expert_ids = jnp.arange(experts, dtype=jnp.int32)
    onehot = (route_col[:, None] == expert_ids).astype(jnp.int32)
    earlier = jnp.cumsum(onehot, axis=0) - onehot
    slot = jnp.sum(onehot * earlier, axis=1)
    position = route_col * padded + slot
    return (jnp.arange(experts * padded, dtype=jnp.int32)[:, None] == position[None, :])


def per_device(inputs, routes, router_scores, cotangent, w_gate, w_up, w_down):
    experts, n, pipes = lax.axis_size("expert"), lax.axis_size("dp"), lax.axis_size("pipe")
    tokens, width = inputs.shape[1:]
    depth = w_gate.shape[2]
    capacity = max(2, tokens * 5 // (4 * experts))
    cap = -(-capacity // 16) * 16
    rows = experts * cap
    route_col = routes[0, :, 0]
    behind = lax.ppermute(route_col, "pipe", [(i + 1, i) for i in range(pipes - 1)])
    table = tables(route_col, experts, capacity, cap)
    following = tables(behind, experts, capacity, cap).astype(jnp.bfloat16)
    raised = jnp.exp(router_scores[0])
    weights = raised / jnp.sum(raised, axis=1, keepdims=True)
    gate = lax.optimization_barrier(weights[:, 0:1].astype(jnp.bfloat16)).astype(jnp.float32)

    vmem = pl.BlockSpec(memory_space=pltpu.VMEM)
    half, full = jnp.bfloat16, jnp.float32
    dma = pltpu.SemaphoreType.DMA
    grad = jax.ShapeDtypeStruct((depth, width), half)
    handed, grad_gate, grad_up, grad_down, sums = pl.pallas_call(
        functools.partial(kernel, (pipes, experts, n, cap, depth)),
        out_shape=(
            jax.ShapeDtypeStruct((tokens, width), half), grad, grad, grad,
            jax.ShapeDtypeStruct((rows, 128), full),
        ),
        in_specs=[vmem] * 8,
        out_specs=(vmem,) * 5,
        scratch_shapes=[
            pltpu.VMEM((2, rows, width), half),
            pltpu.VMEM((n * rows, width), half),
            pltpu.VMEM((n * rows, width), half),
            pltpu.VMEM((n * rows, width), half),
            pltpu.VMEM(((n + 1) * rows, width), half),
            pltpu.VMEM((rows, width), half),
            pltpu.VMEM((n * rows, depth), half),
            pltpu.VMEM((n * rows, depth), half),
            pltpu.VMEM((n * rows, depth), half),
            pltpu.VMEM((n * rows, 128), full),
            pltpu.VMEM((n, rows, 128), full),
            dma((2, experts)), dma((2, experts)),
            dma((2, n, 2, 2)), dma((2, n, 2, 2)),
            dma((n, 2)), dma((n + 1, 2)),
            dma((experts, n)), dma((experts, n)),
            dma((experts,)), dma((experts,)),
        ],
        compiler_params=pltpu.CompilerParams(
            collective_id=0, has_side_effects=True, vmem_limit_bytes=62 * 1024 * 1024
        ),
    )(
        inputs[0], cotangent[0], gate, table.astype(half), following,
        w_gate[0, 0], w_up[0, 0], w_down[0, 0],
    )
    gate_grad = jnp.sum(jnp.where(table, sums[:, 0:1], 0.0), axis=0)[:, None] / gate
    is_first = (jnp.arange(router_scores.shape[2]) == 0).astype(full)
    score_grad = gate_grad * weights[:, 0:1] * (is_first - weights)
    return (
        score_grad[None],
        handed[None],
        grad_gate[None, None],
        grad_up[None, None],
        grad_down[None, None],
    )


def solution(mesh):
    rows = P("pipe", ("expert", "dp"), None)
    mats = P("pipe", "expert", "dp", None)
    return jax.shard_map(
        per_device, mesh=mesh, in_specs=(rows,) * 4 + (mats,) * 3,
        out_specs=(rows, rows, mats, mats, mats), check_vma=False,
    )
```

```python
import functools

import jax
import jax.numpy as jnp
from jax import lax
from jax.experimental import pallas as pl
from jax.experimental.pallas import tpu as pltpu
from jax.sharding import PartitionSpec as P

MESH = pl.DeviceIdType.MESH
NT = (((1,), (1,)), ((), ()))
TN = (((0,), (0,)), ((), ()))


def compute_order(k, n):
    order = [k]
    for d in range(1, n):
        order += [b for b in (k - d, k + d) if 0 <= b < n]
    if n > 2 and k in (0, n - 1):
        order = [k] + order[2:] + [order[1]]
    if k >= n // 2 and 0 < k < n - 1:
        order = [k]
        for d in range(1, n):
            order += [b for b in (k + d, k - d) if 0 <= b < n]
    return order


def finish_order(k, n):
    if k in (0, n - 1):
        return []
    rightward = list(range(k + 1, n))
    leftward = list(range(k - 1, -1, -1))
    return rightward + leftward if k < n // 2 else leftward + rightward


def kernel(
    dims, x_ref, up_ref, gate_ref, tab_ref, nxt_ref, wg_ref, wu_ref, wd_ref,
    out_ref, gg_ref, gu_ref, gd_ref, s_ref,
    xd, yd, tabs, stage, xb, yb, dxb, dxr, hrecv, act, pg, pu, sbuf, srecv,
    t_send, t_recv, e_send, e_recv, f_send, f_recv, r_send, r_recv, s_send, s_recv, h_send, h_recv,
):
    pipes, experts, n, cap, depth = dims
    rows = experts * cap
    p, y, z = lax.axis_index("pipe"), lax.axis_index("expert"), lax.axis_index("dp")
    tokens, width = x_ref.shape

    def peer(de, dz):
        return lax.rem(y + de, experts), lax.rem(z + dz, n)

    others = [(de, dz) for de in range(experts) for dz in range(n) if (de, dz) != (0, 0)]

    barrier = pltpu.get_barrier_semaphore()
    for de, dz in others:
        ey, ez = peer(de, dz)
        pl.semaphore_signal(barrier, inc=1, device_id=(p, ey, ez), device_id_type=MESH)

    @pl.when(p > 0)
    def _():
        for e in range(experts):
            pl.semaphore_signal(barrier, inc=1, device_id=(p - 1, e, z), device_id_type=MESH)

    @pl.when(p < pipes - 1)
    def _():
        for e in range(experts):
            pl.semaphore_signal(barrier, inc=1, device_id=(p + 1, e, z), device_id_type=MESH)

    begin, length = (0, cap), (cap, rows - cap)

    def piece(ref, b, q):
        return ref.at[pl.ds(pl.multiple_of(b * rows + begin[q], 16), length[q])]

    step = min(512, width)
    slots = stage.shape[0] // length[1]

    def dense(ref, b):
        return ref.at[pl.ds(pl.multiple_of(b * tokens, 16), tokens)]

    def held(t, b, i):
        return (dxb, b * rows + cap) if t == 0 else (stage, i % slots * length[1])

    def exchange(t, b, i, de):
        ref, off = held(t, b, i)
        return pltpu.make_async_remote_copy(
            src_ref=ref.at[pl.ds(pl.multiple_of(off + (de - 1) * cap, 16), cap)],
            dst_ref=(xb, yb)[t].at[pl.ds(pl.multiple_of(b * rows + (experts - de) * cap, 16), cap)],
            send_sem=e_send.at[t, i, de], recv_sem=e_recv.at[t, i, de],
            device_id=(p, lax.rem(y + de, experts), z), device_id_type=MESH,
        )

    def pack(t, b, i):
        if t and i >= slots:
            for de in range(1, experts):
                exchange(t, b, i - slots, de).wait_send()
        source = dense((xd, yd)[t], b) if i or t else x_ref
        ref, off = held(t, b, i)
        tab = tabs[b]

        def tile(j, c):
            cols = pl.ds(pl.multiple_of(j * step, step), step)
            vals = jnp.dot(tab, source[:, cols], preferred_element_type=jnp.float32).astype(jnp.bfloat16)
            (xb, yb)[t][pl.ds(pl.multiple_of(b * rows, 16), cap), cols] = vals[:cap]
            ref[pl.ds(pl.multiple_of(off, 16), length[1]), cols] = vals[cap:]
            return c

        lax.fori_loop(0, width // step, tile, 0)
        for de in range(1, experts):
            exchange(t, b, i, de).start()

    def scale(j, c):
        cols = pl.ds(pl.multiple_of(j * step, step), step)
        vals = (gate_ref[...] * up_ref[:, cols].astype(jnp.float32)).astype(jnp.bfloat16)
        yd[pl.ds(pl.multiple_of(z * tokens, 16), tokens), cols] = vals
        return c

    def table_copy(dz):
        return pltpu.make_async_remote_copy(
            src_ref=tab_ref, dst_ref=tabs.at[z], send_sem=t_send.at[dz], recv_sem=t_recv.at[dz],
            device_id=(p, y, lax.rem(z + dz, n)), device_id_type=MESH,
        )

    tabs[z] = tab_ref[...]
    lax.fori_loop(0, width // step, scale, 0)
    around = (p > 0).astype(jnp.int32) + (p < pipes - 1).astype(jnp.int32)
    pl.semaphore_wait(barrier, len(others) + experts * around)

    def forward(b, t, side, own=False):
        there = dense((xd, yd)[t], b)
        return pltpu.make_async_remote_copy(
            src_ref=x_ref if own and t == 0 else there, dst_ref=there,
            send_sem=f_send.at[side, b, t], recv_sem=f_recv.at[side, b, t],
            device_id=(p, y, z + (1 if side else -1)), device_id_type=MESH,
        )

    def running(k, b, q, side):
        slot = n if (not side and b == k - 1) else b
        return pltpu.make_async_remote_copy(
            src_ref=piece(dxb, b, q), dst_ref=piece(dxr, slot, q),
            send_sem=r_send.at[b, q], recv_sem=r_recv.at[slot, q],
            device_id=(p, y, z + (1 if side else -1)), device_id_type=MESH,
        )

    def taken(slot, q):
        whole = piece(dxr, slot, q)
        pltpu.make_async_copy(whole, whole, r_recv.at[slot, q]).wait()

    def arrive(k, b, t):
        side = 1 if b < k else 0
        forward(b, t, side).wait_recv()
        if side and k < n - 1 or not side and k > 0:
            forward(b, t, side).start()

    def near_end(k, side):
        return n > 2 and (side and k == n - 2 or not side and k == 1)

    def sides(k):
        return ([1] if k < n - 1 else []) + ([0] if k > 0 else [])

    for t in range(2):
        for k in range(n):
            @pl.when(z == k)
            def _():
                for side in sides(k):
                    if t == 0 or not near_end(k, side):
                        forward(k, t, side, True).start()
    for dz in range(1, n):
        table_copy(dz).start()

    def work(b, start, size):
        off = pl.multiple_of(b * rows + start, 16)
        here = pl.ds(off, size)
        deep = min(1024, width)

        def into(j, c):
            cols = pl.ds(pl.multiple_of(j * deep, deep), deep)
            xt, yt = xb[here, cols], yb[here, cols]
            g, u, a = c
            g = g + lax.dot_general(xt, wg_ref[:, cols], NT, preferred_element_type=jnp.float32)
            u = u + lax.dot_general(xt, wu_ref[:, cols], NT, preferred_element_type=jnp.float32)
            a = a + lax.dot_general(yt, wd_ref[:, cols], NT, preferred_element_type=jnp.float32)
            return g, u, a

        zero = jnp.zeros((size, depth), jnp.float32)
        g, u, a = lax.fori_loop(0, width // deep, into, (zero, zero, zero))
        sig = 1.0 / (1.0 + jnp.exp(-g))
        silu = g * sig
        hidden = (silu * u).astype(jnp.bfloat16)
        act[here] = hidden
        total = jnp.sum(hidden.astype(jnp.float32) * a, axis=1, keepdims=True)
        sbuf[here] = jnp.broadcast_to(total, (size, 128))
        dg = (a * u * sig * (1.0 + g * (1.0 - sig))).astype(jnp.bfloat16)
        du = (a * silu).astype(jnp.bfloat16)
        pg[here] = dg
        pu[here] = du

        def back(j, c):
            cols = pl.ds(pl.multiple_of(j * step, step), step)
            part = jnp.dot(pg[here], wg_ref[:, cols], preferred_element_type=jnp.float32)
            part = part + jnp.dot(pu[here], wu_ref[:, cols], preferred_element_type=jnp.float32)
            dxb[here, cols] = part.astype(jnp.bfloat16)
            return c

        lax.fori_loop(0, width // step, back, 0)

    orders = [compute_order(k, n) for k in range(n)]
    def place(ks, i):
        b = 0
        for k in ks:
            b = b + (z == k).astype(jnp.int32) * orders[k][i]
        return b

    def come(ks, t, indices):
        for k in ks:
            @pl.when(z == k)
            def _():
                for i in indices:
                    arrive(k, orders[k][i], t)

    def join(b, i):
        for de in range(1, experts):
            exchange(0, b, i, de).wait_send()
            for t in range(2):
                exchange(t, b, i, de).wait_recv()

    def part(ks, i, q):
        b = place(ks, i)
        if q:
            join(b, i)
        work(b, begin[q], length[q])
        if i:
            for k in ks:
                if k in (0, n - 1):
                    @pl.when((z == k) & (p > 0))
                    def _():
                        running(k, orders[k][i], q, 0 if k else 1).start()

    def whole(ks, i):
        b = place(ks, i)
        join(b, i)
        work(b, 0, rows)

    def tables_here():
        for dz in range(1, n):
            table_copy(dz).wait_recv()

    ends, middle = sorted({0, n - 1}), list(range(1, n - 1))

    @pl.when((z == 0) | (z == n - 1))
    def _():
        for t in range(2):
            pack(t, place(ends, 0), 0)
        tables_here()
        if n > 2:
            come(ends, 0, [n - 1])
            pack(0, place(ends, n - 1), n - 1)
        for i in range(1, n - 1):
            for t in range(2):
                come(ends, t, [i])
                pack(t, place(ends, i), i)
            if i == 1:
                whole(ends, 0)
            part(ends, i, 0)
            part(ends, i, 1)
        for t in range(2) if n == 2 else (1,):
            come(ends, t, [n - 1])
            pack(t, place(ends, n - 1), n - 1)
        if n == 2:
            whole(ends, 0)
        part(ends, n - 1, 0)
        part(ends, n - 1, 1)

    if middle:
        @pl.when((z > 0) & (z < n - 1))
        def _():
            def release():
                for k in middle:
                    @pl.when(z == k)
                    def _():
                        for side in sides(k):
                            if near_end(k, side):
                                forward(k, 1, side, True).start()

            for t in range(2):
                pack(t, place(middle, 0), 0)
            tables_here()
            for t in range(2):
                come(middle, t, [1, 2])
                for i in (1, 2):
                    pack(t, place(middle, i), i)
            if n == 3:
                release()
            whole(middle, 0)
            due = [1, 2]
            for i in range(3, n):
                come(middle, 0, [i])
                pack(0, place(middle, i), i)
                for c in due:
                    whole(middle, c)
                come(middle, 1, [i])
                if i == n - 1:
                    release()
                pack(1, place(middle, i), i)
                due = [i]
            for c in due:
                if c == n - 1:
                    part(middle, c, 0)
                    part(middle, c, 1)
                else:
                    whole(middle, c)

    def tell(de, dz):
        ey, ez = peer(de, dz)
        return pltpu.make_async_remote_copy(
            src_ref=sbuf.at[pl.ds(pl.multiple_of(ez * rows + de * cap, 16), cap)],
            dst_ref=srecv.at[z, pl.ds((experts - de) % experts * cap, cap)],
            send_sem=s_send.at[de, dz], recv_sem=s_recv.at[de, dz],
            device_id=(p, ey, ez), device_id_type=MESH,
        )

    for de, dz in others:
        tell(de, dz).start()
    srecv[z, :cap] = sbuf[
        pl.ds(pl.multiple_of(z * rows, 16), cap)
    ]

    def weights(j, c):
        cols = pl.ds(pl.multiple_of(j * step, step), step)
        yt, xt = yb[:, cols], xb[:, cols]
        gd_ref[:, cols] = lax.dot_general(act[...], yt, TN, preferred_element_type=jnp.float32).astype(jnp.bfloat16)
        gg_ref[:, cols] = lax.dot_general(pg[...], xt, TN, preferred_element_type=jnp.float32).astype(jnp.bfloat16)
        gu_ref[:, cols] = lax.dot_general(pu[...], xt, TN, preferred_element_type=jnp.float32).astype(jnp.bfloat16)
        return c

    lax.fori_loop(0, width // step, weights, 0)

    def add(b, slots, q):
        def some(j, c):
            here = pl.ds(pl.multiple_of(b * rows + begin[q] + j * 16, 16), 16)
            total = dxb[here].astype(jnp.float32)
            for slot in slots:
                there = pl.ds(pl.multiple_of(slot * rows + begin[q] + j * 16, 16), 16)
                total = total + dxr[there].astype(jnp.float32)
            dxb[here] = total.astype(jnp.bfloat16)
            return c

        lax.fori_loop(0, length[q] // 16, some, 0)

    def hand(de):
        return pltpu.make_async_remote_copy(
            src_ref=dxb.at[pl.ds(pl.multiple_of(z * rows + de * cap, 16), cap)],
            dst_ref=hrecv.at[pl.ds((experts - de) % experts * cap, cap)],
            send_sem=h_send.at[de], recv_sem=h_recv.at[de],
            device_id=(p - 1, lax.rem(y + de, experts), z), device_id_type=MESH,
        )

    for k in range(n):
        @pl.when((z == k) & (p > 0))
        def _():
            for b in finish_order(k, n):
                for q in (0, 1):
                    taken(b, q)
                    add(b, [b], q)
                    running(k, b, q, 1 if b > k else 0).start()
            ends_in = ([k] if k > 0 else []) + ([n] if k < n - 1 else [])
            for q in (0, 1):
                for slot in ends_in:
                    taken(slot, q)
                add(k, ends_in, q)
                for de in (range(1, experts) if q else (0,)):
                    hand(de).start()

    for de, dz in others:
        tell(de, dz).wait_recv()
    total = srecv[0]
    for k in range(1, n):
        total = total + srecv[k]
    s_ref[...] = total

    @pl.when(p < pipes - 1)
    def _():
        for e in range(experts):
            hand(e).wait_recv()

        def tile(j, c):
            cols = pl.ds(pl.multiple_of(j * step, step), step)
            out_ref[:, cols] = lax.dot_general(
                nxt_ref[...], hrecv[:, cols], TN, preferred_element_type=jnp.float32
            ).astype(jnp.bfloat16)
            return c

        lax.fori_loop(0, width // step, tile, 0)

    @pl.when(p == pipes - 1)
    def _():
        out_ref[...] = jnp.zeros_like(out_ref)

    for i in range(max(0, n - slots), n):
        for de in range(1, experts):
            exchange(1, 0, i, de).wait_send()
    for dz in range(1, n):
        table_copy(dz).wait_send()
    for de, dz in others:
        tell(de, dz).wait_send()
    for k in range(n):
        @pl.when(z == k)
        def _():
            for b in range(n):
                for side in sides(k):
                    if b == k or (b < k and side) or (b > k and not side):
                        for t in range(2):
                            forward(b, t, side, b == k).wait_send()

        @pl.when((z == k) & (p > 0))
        def _():
            for b in range(n):
                if b != k:
                    for q in (0, 1):
                        running(k, b, q, 1 if b > k else 0).wait_send()

    @pl.when(p > 0)
    def _():
        for de in range(experts):
            hand(de).wait_send()


def tables(route_col, experts, padded):
    expert_ids = jnp.arange(experts, dtype=jnp.int32)
    onehot = (route_col[:, None] == expert_ids).astype(jnp.int32)
    earlier = jnp.cumsum(onehot, axis=0) - onehot
    slot = jnp.sum(onehot * earlier, axis=1)
    position = (route_col - lax.axis_index("expert") + experts) % experts * padded + slot
    return (jnp.arange(experts * padded, dtype=jnp.int32)[:, None] == position[None, :])


def per_device(inputs, routes, router_scores, cotangent, w_gate, w_up, w_down):
    experts, n, pipes = lax.axis_size("expert"), lax.axis_size("dp"), lax.axis_size("pipe")
    tokens, width = inputs.shape[1:]
    depth = w_gate.shape[2]
    capacity = max(2, tokens * 5 // (4 * experts))
    cap = -(-capacity // 16) * 16
    rows = experts * cap
    route_col = routes[0, :, 0]
    behind = lax.ppermute(route_col, "pipe", [(i + 1, i) for i in range(pipes - 1)])
    table = tables(route_col, experts, cap)
    following = tables(behind, experts, cap).astype(jnp.bfloat16)
    raised = jnp.exp(router_scores[0])
    weights = raised / jnp.sum(raised, axis=1, keepdims=True)
    gate = lax.optimization_barrier(weights[:, 0:1].astype(jnp.bfloat16)).astype(jnp.float32)

    vmem = pl.BlockSpec(memory_space=pltpu.VMEM)
    half, full = jnp.bfloat16, jnp.float32
    dma = pltpu.SemaphoreType.DMA
    grad = jax.ShapeDtypeStruct((depth, width), half)
    handed, grad_gate, grad_up, grad_down, sums = pl.pallas_call(
        functools.partial(kernel, (pipes, experts, n, cap, depth)),
        out_shape=(
            jax.ShapeDtypeStruct((tokens, width), half), grad, grad, grad,
            jax.ShapeDtypeStruct((rows, 128), full),
        ),
        in_specs=[vmem] * 8,
        out_specs=(vmem,) * 5,
        scratch_shapes=[
            pltpu.VMEM((n * tokens, width), half),
            pltpu.VMEM((n * tokens, width), half),
            pltpu.VMEM((n, rows, tokens), half),
            pltpu.VMEM((min(n, max(1, 320 // (rows - cap))) * (rows - cap), width), half),
            pltpu.VMEM((n * rows, width), half),
            pltpu.VMEM((n * rows, width), half),
            pltpu.VMEM((n * rows, width), half),
            pltpu.VMEM(((n + 1) * rows, width), half),
            pltpu.VMEM((rows, width), half),
            pltpu.VMEM((n * rows, depth), half),
            pltpu.VMEM((n * rows, depth), half),
            pltpu.VMEM((n * rows, depth), half),
            pltpu.VMEM((n * rows, 128), full),
            pltpu.VMEM((n, rows, 128), full),
            dma((n,)), dma((n,)),
            dma((2, n, experts)), dma((2, n, experts)),
            dma((2, n, 2)), dma((2, n, 2)),
            dma((n, 2)), dma((n + 1, 2)),
            dma((experts, n)), dma((experts, n)),
            dma((experts,)), dma((experts,)),
        ],
        compiler_params=pltpu.CompilerParams(
            collective_id=0, has_side_effects=True, vmem_limit_bytes=63 * 1024 * 1024
        ),
    )(
        inputs[0], cotangent[0], gate, table.astype(half), following,
        w_gate[0, 0], w_up[0, 0], w_down[0, 0],
    )
    gate_grad = jnp.sum(jnp.where(table, sums[:, 0:1], 0.0), axis=0)[:, None] / gate
    is_first = (jnp.arange(router_scores.shape[2]) == 0).astype(full)
    score_grad = gate_grad * weights[:, 0:1] * (is_first - weights)
    return (
        score_grad[None],
        handed[None],
        grad_gate[None, None],
        grad_up[None, None],
        grad_down[None, None],
    )


def solution(mesh):
    rows = P("pipe", ("expert", "dp"), None)
    mats = P("pipe", "expert", "dp", None)
    return jax.shard_map(
        per_device, mesh=mesh, in_specs=(rows,) * 4 + (mats,) * 3,
        out_specs=(rows, rows, mats, mats, mats), check_vma=False,
    )
```

```python
import functools

import jax
import jax.numpy as jnp
from jax import lax
from jax.experimental import pallas as pl
from jax.experimental.pallas import tpu as pltpu
from jax.sharding import PartitionSpec as P

MESH = pl.DeviceIdType.MESH
NT = (((1,), (1,)), ((), ()))
TN = (((0,), (0,)), ((), ()))


def compute_order(k, n):
    order = [k]
    for d in range(1, n):
        order += [b for b in (k - d, k + d) if 0 <= b < n]
    if n > 2 and k in (0, n - 1):
        order = [k] + order[2:] + [order[1]]
    if k >= n // 2 and 0 < k < n - 1:
        order = [k]
        for d in range(1, n):
            order += [b for b in (k + d, k - d) if 0 <= b < n]
    return order


def finish_order(k, n):
    if k in (0, n - 1):
        return []
    rightward = list(range(k + 1, n))
    leftward = list(range(k - 1, -1, -1))
    return rightward + leftward if k < n // 2 else leftward + rightward


def kernel(
    dims, x_ref, up_ref, gate_ref, tab_ref, wg_ref, wu_ref, wd_ref,
    hrecv, gg_ref, gu_ref, gd_ref, s_ref,
    stage, xb, yb, dxb, dxr, act, pg, pu, turned, sbuf, srecv,
    ey_send, ey_recv, f_send, f_recv, r_send, r_recv, s_send, s_recv, h_send, h_recv,
):
    pipes, experts, n, cap, depth = dims
    rows = experts * cap
    p, y, z = lax.axis_index("pipe"), lax.axis_index("expert"), lax.axis_index("dp")
    tokens, width = x_ref.shape

    def peer(de, dz):
        return lax.rem(y + de, experts), lax.rem(z + dz, n)

    others = [(de, dz) for de in range(experts) for dz in range(n) if (de, dz) != (0, 0)]

    barrier = pltpu.get_barrier_semaphore()
    for de, dz in others:
        ey, ez = peer(de, dz)
        pl.semaphore_signal(barrier, inc=1, device_id=(p, ey, ez), device_id_type=MESH)

    @pl.when(p > 0)
    def _():
        for e in range(experts):
            pl.semaphore_signal(barrier, inc=1, device_id=(p - 1, e, z), device_id_type=MESH)

    @pl.when(p < pipes - 1)
    def _():
        for e in range(experts):
            pl.semaphore_signal(barrier, inc=1, device_id=(p + 1, e, z), device_id_type=MESH)

    begin, length = (0, cap), (cap, rows - cap)

    def piece(ref, b, q):
        return ref.at[pl.ds(pl.multiple_of(b * rows + begin[q], 16), length[q])]

    tab = tab_ref[...]
    step = min(512, width)

    def pack(t, buffer):
        def tile(j, c):
            cols = pl.ds(pl.multiple_of(j * step, step), step)
            if t == 0:
                vals = x_ref[:, cols]
            else:
                vals = (gate_ref[...] * up_ref[:, cols].astype(jnp.float32)).astype(jnp.bfloat16)
            stage[t, :, cols] = jnp.dot(tab, vals, preferred_element_type=jnp.float32).astype(jnp.bfloat16)
            return c

        lax.fori_loop(0, width // step, tile, 0)

    def exchange(t, buffer, de):
        e = lax.rem(y + de, experts)
        return pltpu.make_async_remote_copy(
            src_ref=stage.at[t, pl.ds(pl.multiple_of(e * cap, 16), cap)],
            dst_ref=buffer.at[pl.ds(pl.multiple_of(z * rows + (experts - de) * cap, 16), cap)],
            send_sem=ey_send.at[t, de], recv_sem=ey_recv.at[t, de],
            device_id=(p, e, z), device_id_type=MESH,
        )

    pack(0, xb)
    around = (p > 0).astype(jnp.int32) + (p < pipes - 1).astype(jnp.int32)
    pl.semaphore_wait(barrier, len(others) + experts * around)

    def forward(b, t, q, side):
        buffer = (xb, yb)[t]
        return pltpu.make_async_remote_copy(
            src_ref=piece(buffer, b, q), dst_ref=piece(buffer, b, q),
            send_sem=f_send.at[side, b, t, q], recv_sem=f_recv.at[side, b, t, q],
            device_id=(p, y, z + (1 if side else -1)), device_id_type=MESH,
        )

    def running(k, b, q, side):
        slot = n if (not side and b == k - 1) else b
        return pltpu.make_async_remote_copy(
            src_ref=piece(dxb, b, q), dst_ref=piece(dxr, slot, q),
            send_sem=r_send.at[b, q], recv_sem=r_recv.at[slot, q],
            device_id=(p, y, z + (1 if side else -1)), device_id_type=MESH,
        )

    def taken(slot, q):
        whole = piece(dxr, slot, q)
        pltpu.make_async_copy(whole, whole, r_recv.at[slot, q]).wait()

    def arrive(k, b, t, q):
        side = 1 if b < k else 0
        forward(b, t, q, side).wait_recv()
        if side and k < n - 1 or not side and k > 0:
            forward(b, t, q, side).start()

    def near_end(k, side):
        return n > 2 and (side and k == n - 2 or not side and k == 1)

    def sides(k):
        return ([1] if k < n - 1 else []) + ([0] if k > 0 else [])

    def depart(t, q):
        for k in range(n):
            @pl.when(z == k)
            def _():
                for side in sides(k):
                    if t == 0 or not near_end(k, side):
                        forward(k, t, q, side).start()

    for t, buffer in ((0, xb), (1, yb)):
        if t:
            pack(1, yb)
        for de in range(1, experts):
            exchange(t, buffer, de).start()
        buffer[pl.ds(pl.multiple_of(z * rows, 16), cap)] = stage[t, pl.ds(pl.multiple_of(y * cap, 16), cap)]
        depart(t, 0)
    for t, buffer in ((0, xb), (1, yb)):
        for de in range(1, experts):
            exchange(t, buffer, de).wait_recv()
        depart(t, 1)

    def work(b, start, size):
        off = pl.multiple_of(b * rows + start, 16)
        here = pl.ds(off, size)
        deep = min(1024, width)

        def into(j, c):
            cols = pl.ds(pl.multiple_of(j * deep, deep), deep)
            xt, yt = xb[here, cols], yb[here, cols]
            g, u, a = c
            g = g + lax.dot_general(xt, wg_ref[:, cols], NT, preferred_element_type=jnp.float32)
            u = u + lax.dot_general(xt, wu_ref[:, cols], NT, preferred_element_type=jnp.float32)
            a = a + lax.dot_general(yt, wd_ref[:, cols], NT, preferred_element_type=jnp.float32)
            return g, u, a

        zero = jnp.zeros((size, depth), jnp.float32)
        g, u, a = lax.fori_loop(0, width // deep, into, (zero, zero, zero))
        sig = 1.0 / (1.0 + jnp.exp(-g))
        silu = g * sig
        hidden = (silu * u).astype(jnp.bfloat16)
        act[here] = hidden
        total = jnp.sum(hidden.astype(jnp.float32) * a, axis=1, keepdims=True)
        sbuf[here] = jnp.broadcast_to(total, (size, 128))
        dg = (a * u * sig * (1.0 + g * (1.0 - sig))).astype(jnp.bfloat16)
        du = (a * silu).astype(jnp.bfloat16)
        pg[here] = dg
        pu[here] = du

        def back(j, c):
            cols = pl.ds(pl.multiple_of(j * step, step), step)
            part = jnp.dot(pg[here], wg_ref[:, cols], preferred_element_type=jnp.float32)
            part = part + jnp.dot(pu[here], wu_ref[:, cols], preferred_element_type=jnp.float32)
            dxb[here, cols] = part.astype(jnp.bfloat16)
            return c

        lax.fori_loop(0, width // step, back, 0)

    orders = [compute_order(k, n) for k in range(n)]
    both = ((0, 0), (1, 0), (0, 1), (1, 1))
    for i in range(n):
        b = 0
        for k in range(n):
            b = b + (z == k).astype(jnp.int32) * orders[k][i]
        last = n > 1 and i == n - 1
        for part in ((0, 1) if i else (None,)):
            items = [item for item in both if part is None or item[1] == part]
            for k in range(n):
                @pl.when(z == k)
                def _():
                    c = orders[k][i]
                    if i == 0:
                        if 0 < k < n - 1:
                            for t in range(2):
                                for e in (k - 1, k + 1):
                                    arrive(k, e, t, 0)
                    elif k in (0, n - 1):
                        for t, q in items:
                            arrive(k, c, t, q)
                    else:
                        d = abs(c - k)
                        pair = [e for e in (k - d, k + d) if 0 <= e < n]
                        if last and len(pair) == 1 or not last and all(orders[k].index(e) >= i for e in pair):
                            for t, q in items if i > 1 or part else ():
                                for e in pair:
                                    arrive(k, e, t, q)
                        if last and part == 1:
                            for side in sides(k):
                                if near_end(k, side):
                                    forward(k, 1, 0, side).start()
            if part is None:
                work(b, 0, rows)
            else:
                work(b, begin[part], length[part])
            if last and part == 1:
                for k in range(n):
                    for side in sides(k):
                        if near_end(k, side):
                            @pl.when(z == k)
                            def _():
                                forward(k, 1, 1, side).start()
            if i:
                for k in (0, n - 1):
                    @pl.when((z == k) & (p > 0))
                    def _():
                        for q in (0, 1) if part is None else (part,):
                            running(k, orders[k][i], q, 0 if k else 1).start()

    def tell(de, dz):
        ey, ez = peer(de, dz)
        return pltpu.make_async_remote_copy(
            src_ref=sbuf.at[pl.ds(pl.multiple_of(ez * rows + de * cap, 16), cap)],
            dst_ref=srecv.at[z, pl.ds(pl.multiple_of(y * cap, 16), cap)],
            send_sem=s_send.at[de, dz], recv_sem=s_recv.at[de, dz],
            device_id=(p, ey, ez), device_id_type=MESH,
        )

    for de, dz in others:
        tell(de, dz).start()
    srecv[z, pl.ds(pl.multiple_of(y * cap, 16), cap)] = sbuf[
        pl.ds(pl.multiple_of(z * rows, 16), cap)
    ]

    for m, ref in enumerate((act, pg, pu)):
        turned[m] = ref[...].T

    def weights(j, c):
        cols = pl.ds(pl.multiple_of(j * step, step), step)
        yt, xt = yb[:, cols], xb[:, cols]
        gd_ref[:, cols] = jnp.dot(turned[0], yt, preferred_element_type=jnp.float32).astype(jnp.bfloat16)
        gg_ref[:, cols] = jnp.dot(turned[1], xt, preferred_element_type=jnp.float32).astype(jnp.bfloat16)
        gu_ref[:, cols] = jnp.dot(turned[2], xt, preferred_element_type=jnp.float32).astype(jnp.bfloat16)
        return c

    lax.fori_loop(0, width // step, weights, 0)

    def add(b, slots, q):
        def some(j, c):
            here = pl.ds(pl.multiple_of(b * rows + begin[q] + j * 16, 16), 16)
            total = dxb[here].astype(jnp.float32)
            for slot in slots:
                there = pl.ds(pl.multiple_of(slot * rows + begin[q] + j * 16, 16), 16)
                total = total + dxr[there].astype(jnp.float32)
            dxb[here] = total.astype(jnp.bfloat16)
            return c

        lax.fori_loop(0, length[q] // 16, some, 0)

    def hand(de):
        return pltpu.make_async_remote_copy(
            src_ref=dxb.at[pl.ds(pl.multiple_of(z * rows + de * cap, 16), cap)],
            dst_ref=hrecv.at[pl.ds(pl.multiple_of(y * cap, 16), cap)],
            send_sem=h_send.at[de], recv_sem=h_recv.at[y],
            device_id=(p - 1, lax.rem(y + de, experts), z), device_id_type=MESH,
        )

    for k in range(n):
        @pl.when((z == k) & (p > 0))
        def _():
            for b in finish_order(k, n):
                for q in (0, 1):
                    taken(b, q)
                    add(b, [b], q)
                    running(k, b, q, 1 if b > k else 0).start()
            slots = ([k] if k > 0 else []) + ([n] if k < n - 1 else [])
            for q in (0, 1):
                for slot in slots:
                    taken(slot, q)
                add(k, slots, q)
                for de in (range(1, experts) if q else (0,)):
                    hand(de).start()

    for de, dz in others:
        tell(de, dz).wait_recv()
    total = srecv[0]
    for k in range(1, n):
        total = total + srecv[k]
    s_ref[...] = total

    @pl.when(p < pipes - 1)
    def _():
        for e in range(experts):
            pltpu.make_async_copy(hrecv.at[pl.ds(e * cap, cap)], hrecv.at[pl.ds(e * cap, cap)], h_recv.at[e]).wait()

    @pl.when(p == pipes - 1)
    def _():
        hrecv[...] = jnp.zeros_like(hrecv)

    for t, buffer in ((0, xb), (1, yb)):
        for de in range(1, experts):
            exchange(t, buffer, de).wait_send()
    for de, dz in others:
        tell(de, dz).wait_send()
    for k in range(n):
        @pl.when(z == k)
        def _():
            for b in range(n):
                for side in sides(k):
                    if b == k or (b < k and side) or (b > k and not side):
                        for t, q in both:
                            forward(b, t, q, side).wait_send()

        @pl.when((z == k) & (p > 0))
        def _():
            for b in range(n):
                if b != k:
                    for q in (0, 1):
                        running(k, b, q, 1 if b > k else 0).wait_send()

    @pl.when(p > 0)
    def _():
        for de in range(experts):
            hand(de).wait_send()


def tables(route_col, experts, capacity, padded):
    expert_ids = jnp.arange(experts, dtype=jnp.int32)
    onehot = (route_col[:, None] == expert_ids).astype(jnp.int32)
    earlier = jnp.cumsum(onehot, axis=0) - onehot
    slot = jnp.sum(onehot * earlier, axis=1)
    position = route_col * padded + slot
    return (jnp.arange(experts * padded, dtype=jnp.int32)[:, None] == position[None, :])


def per_device(inputs, routes, router_scores, cotangent, w_gate, w_up, w_down):
    experts, n, pipes = lax.axis_size("expert"), lax.axis_size("dp"), lax.axis_size("pipe")
    tokens, width = inputs.shape[1:]
    depth = w_gate.shape[2]
    capacity = max(2, tokens * 5 // (4 * experts))
    cap = -(-capacity // 16) * 16
    rows = experts * cap
    route_col = routes[0, :, 0]
    behind = lax.ppermute(route_col, "pipe", [(i + 1, i) for i in range(pipes - 1)])
    table = tables(route_col, experts, capacity, cap)
    following = tables(behind, experts, capacity, cap).astype(jnp.bfloat16)
    raised = jnp.exp(router_scores[0])
    weights = raised / jnp.sum(raised, axis=1, keepdims=True)
    gate = lax.optimization_barrier(weights[:, 0:1].astype(jnp.bfloat16)).astype(jnp.float32)

    vmem = pl.BlockSpec(memory_space=pltpu.VMEM)
    half, full = jnp.bfloat16, jnp.float32
    dma = pltpu.SemaphoreType.DMA
    grad = jax.ShapeDtypeStruct((depth, width), half)
    returned, grad_gate, grad_up, grad_down, sums = pl.pallas_call(
        functools.partial(kernel, (pipes, experts, n, cap, depth)),
        out_shape=(
            jax.ShapeDtypeStruct((rows, width), half), grad, grad, grad,
            jax.ShapeDtypeStruct((rows, 128), full),
        ),
        in_specs=[vmem] * 7,
        out_specs=(vmem,) * 5,
        scratch_shapes=[
            pltpu.VMEM((2, rows, width), half),
            pltpu.VMEM((n * rows, width), half),
            pltpu.VMEM((n * rows, width), half),
            pltpu.VMEM((n * rows, width), half),
            pltpu.VMEM(((n + 1) * rows, width), half),
            pltpu.VMEM((n * rows, depth), half),
            pltpu.VMEM((n * rows, depth), half),
            pltpu.VMEM((n * rows, depth), half),
            pltpu.VMEM((3, depth, n * rows), half),
            pltpu.VMEM((n * rows, 128), full),
            pltpu.VMEM((n, rows, 128), full),
            dma((2, experts)), dma((2, experts)),
            dma((2, n, 2, 2)), dma((2, n, 2, 2)),
            dma((n, 2)), dma((n + 1, 2)),
            dma((experts, n)), dma((experts, n)),
            dma((experts,)), dma((experts,)),
        ],
        compiler_params=pltpu.CompilerParams(
            collective_id=0, has_side_effects=True, vmem_limit_bytes=62 * 1024 * 1024
        ),
    )(
        inputs[0], cotangent[0], gate, table.astype(half),
        w_gate[0, 0], w_up[0, 0], w_down[0, 0],
    )
    handed = lax.dot_general(following, returned, TN, preferred_element_type=full).astype(half)
    gate_grad = jnp.sum(jnp.where(table, sums[:, 0:1], 0.0), axis=0)[:, None] / gate
    is_first = (jnp.arange(router_scores.shape[2]) == 0).astype(full)
    score_grad = gate_grad * weights[:, 0:1] * (is_first - weights)
    return (
        score_grad[None],
        handed[None],
        grad_gate[None, None],
        grad_up[None, None],
        grad_down[None, None],
    )


def solution(mesh):
    rows = P("pipe", ("expert", "dp"), None)
    mats = P("pipe", "expert", "dp", None)
    return jax.shard_map(
        per_device, mesh=mesh, in_specs=(rows,) * 4 + (mats,) * 3,
        out_specs=(rows, rows, mats, mats, mats), check_vma=False,
    )
```

```python
import functools

import jax
import jax.numpy as jnp
from jax import lax
from jax.experimental import pallas as pl
from jax.experimental.pallas import tpu as pltpu
from jax.sharding import PartitionSpec as P

MESH = pl.DeviceIdType.MESH
NT = (((1,), (1,)), ((), ()))
TN = (((0,), (0,)), ((), ()))


def compute_order(k, n):
    order = [k]
    for d in range(1, n):
        order += [b for b in (k - d, k + d) if 0 <= b < n]
    if n > 2 and k in (0, n - 1):
        order = [k] + order[2:] + [order[1]]
    if k >= n // 2 and 0 < k < n - 1:
        order = [k]
        for d in range(1, n):
            order += [b for b in (k + d, k - d) if 0 <= b < n]
    return order


def finish_order(k, n):
    if k in (0, n - 1):
        return []
    rightward = list(range(k + 1, n))
    leftward = list(range(k - 1, -1, -1))
    return rightward + leftward if k < n // 2 else leftward + rightward


def kernel(
    dims, x_ref, up_ref, gate_ref, tab_ref, wg_hbm, wu_hbm, wd_hbm,
    hrecv, gg_hbm, gu_hbm, gd_hbm, s_ref,
    wg_ref, wu_ref, wd_ref, gg_ref, gu_ref, gd_ref, w_sem, g_sem,
    stage, xb, yb, dxb, dxr, act, pg, pu, turned, sbuf, srecv,
    ey_send, ey_recv, f_send, f_recv, r_send, r_recv, s_send, s_recv, h_send, h_recv,
):
    pipes, experts, n, cap, depth = dims
    rows = experts * cap
    p, y, z = lax.axis_index("pipe"), lax.axis_index("expert"), lax.axis_index("dp")
    tokens, width = x_ref.shape

    def peer(de, dz):
        return lax.rem(y + de, experts), lax.rem(z + dz, n)

    others = [(de, dz) for de in range(experts) for dz in range(n) if (de, dz) != (0, 0)]

    reads = [
        pltpu.make_async_copy(src, dst, w_sem.at[m])
        for m, (src, dst) in enumerate(((wg_hbm, wg_ref), (wu_hbm, wu_ref), (wd_hbm, wd_ref)))
    ]
    writes = [
        pltpu.make_async_copy(src, dst, g_sem.at[m])
        for m, (src, dst) in enumerate(((gg_ref, gg_hbm), (gu_ref, gu_hbm), (gd_ref, gd_hbm)))
    ]
    for copy in reads:
        copy.start()
    barrier = pltpu.get_barrier_semaphore()
    for de, dz in others:
        ey, ez = peer(de, dz)
        pl.semaphore_signal(barrier, inc=1, device_id=(p, ey, ez), device_id_type=MESH)

    @pl.when(p > 0)
    def _():
        for e in range(experts):
            pl.semaphore_signal(barrier, inc=1, device_id=(p - 1, e, z), device_id_type=MESH)

    @pl.when(p < pipes - 1)
    def _():
        for e in range(experts):
            pl.semaphore_signal(barrier, inc=1, device_id=(p + 1, e, z), device_id_type=MESH)

    begin, length = (0, cap), (cap, rows - cap)

    def piece(ref, b, q):
        return ref.at[pl.ds(pl.multiple_of(b * rows + begin[q], 16), length[q])]

    tab = tab_ref[...]
    step = min(512, width)

    def pack(t, buffer):
        def tile(j, c):
            cols = pl.ds(pl.multiple_of(j * step, step), step)
            if t == 0:
                vals = x_ref[:, cols]
            else:
                vals = (gate_ref[...] * up_ref[:, cols].astype(jnp.float32)).astype(jnp.bfloat16)
            stage[t, :, cols] = jnp.dot(tab, vals, preferred_element_type=jnp.float32).astype(jnp.bfloat16)
            return c

        lax.fori_loop(0, width // step, tile, 0)

    def exchange(t, buffer, de):
        e = lax.rem(y + de, experts)
        return pltpu.make_async_remote_copy(
            src_ref=stage.at[t, pl.ds(pl.multiple_of(e * cap, 16), cap)],
            dst_ref=buffer.at[pl.ds(pl.multiple_of(z * rows + (experts - de) * cap, 16), cap)],
            send_sem=ey_send.at[t, de], recv_sem=ey_recv.at[t, de],
            device_id=(p, e, z), device_id_type=MESH,
        )

    pack(0, xb)
    around = (p > 0).astype(jnp.int32) + (p < pipes - 1).astype(jnp.int32)
    pl.semaphore_wait(barrier, len(others) + experts * around)

    def forward(b, t, q, side):
        buffer = (xb, yb)[t]
        return pltpu.make_async_remote_copy(
            src_ref=piece(buffer, b, q), dst_ref=piece(buffer, b, q),
            send_sem=f_send.at[side, b, t, q], recv_sem=f_recv.at[side, b, t, q],
            device_id=(p, y, z + (1 if side else -1)), device_id_type=MESH,
        )

    def running(k, b, q, side):
        slot = n if (not side and b == k - 1) else b
        return pltpu.make_async_remote_copy(
            src_ref=piece(dxb, b, q), dst_ref=piece(dxr, slot, q),
            send_sem=r_send.at[b, q], recv_sem=r_recv.at[slot, q],
            device_id=(p, y, z + (1 if side else -1)), device_id_type=MESH,
        )

    def taken(slot, q):
        whole = piece(dxr, slot, q)
        pltpu.make_async_copy(whole, whole, r_recv.at[slot, q]).wait()

    def arrive(k, b, t, q):
        side = 1 if b < k else 0
        forward(b, t, q, side).wait_recv()
        if side and k < n - 1 or not side and k > 0:
            forward(b, t, q, side).start()

    def near_end(k, side):
        return n > 2 and (side and k == n - 2 or not side and k == 1)

    def sides(k):
        return ([1] if k < n - 1 else []) + ([0] if k > 0 else [])

    def depart(t, q):
        for k in range(n):
            @pl.when(z == k)
            def _():
                for side in sides(k):
                    if t == 0 or not near_end(k, side):
                        forward(k, t, q, side).start()

    for t, buffer in ((0, xb), (1, yb)):
        if t:
            pack(1, yb)
        for de in range(1, experts):
            exchange(t, buffer, de).start()
        buffer[pl.ds(pl.multiple_of(z * rows, 16), cap)] = stage[t, pl.ds(pl.multiple_of(y * cap, 16), cap)]
        depart(t, 0)
    for t, buffer in ((0, xb), (1, yb)):
        for de in range(1, experts):
            exchange(t, buffer, de).wait_recv()
        depart(t, 1)

    def work(b, start, size):
        off = pl.multiple_of(b * rows + start, 16)
        here = pl.ds(off, size)
        deep = min(1024, width)

        def into(j, c):
            cols = pl.ds(pl.multiple_of(j * deep, deep), deep)
            xt, yt = xb[here, cols], yb[here, cols]
            g, u, a = c
            g = g + lax.dot_general(xt, wg_ref[:, cols], NT, preferred_element_type=jnp.float32)
            u = u + lax.dot_general(xt, wu_ref[:, cols], NT, preferred_element_type=jnp.float32)
            a = a + lax.dot_general(yt, wd_ref[:, cols], NT, preferred_element_type=jnp.float32)
            return g, u, a

        zero = jnp.zeros((size, depth), jnp.float32)
        g, u, a = lax.fori_loop(0, width // deep, into, (zero, zero, zero))
        sig = 1.0 / (1.0 + jnp.exp(-g))
        silu = g * sig
        hidden = (silu * u).astype(jnp.bfloat16)
        act[here] = hidden
        total = jnp.sum(hidden.astype(jnp.float32) * a, axis=1, keepdims=True)
        sbuf[here] = jnp.broadcast_to(total, (size, 128))
        dg = (a * u * sig * (1.0 + g * (1.0 - sig))).astype(jnp.bfloat16)
        du = (a * silu).astype(jnp.bfloat16)
        pg[here] = dg
        pu[here] = du

        def back(j, c):
            cols = pl.ds(pl.multiple_of(j * step, step), step)
            part = jnp.dot(pg[here], wg_ref[:, cols], preferred_element_type=jnp.float32)
            part = part + jnp.dot(pu[here], wu_ref[:, cols], preferred_element_type=jnp.float32)
            dxb[here, cols] = part.astype(jnp.bfloat16)
            return c

        lax.fori_loop(0, width // step, back, 0)

    orders = [compute_order(k, n) for k in range(n)]
    for copy in reads:
        copy.wait()
    both = ((0, 0), (1, 0), (0, 1), (1, 1))
    for i in range(n):
        b = 0
        for k in range(n):
            b = b + (z == k).astype(jnp.int32) * orders[k][i]
        last = n > 1 and i == n - 1
        for part in ((0, 1) if i else (None,)):
            items = [item for item in both if part is None or item[1] == part]
            for k in range(n):
                @pl.when(z == k)
                def _():
                    c = orders[k][i]
                    if i == 0:
                        if 0 < k < n - 1:
                            for t in range(2):
                                for e in (k - 1, k + 1):
                                    arrive(k, e, t, 0)
                    elif k in (0, n - 1):
                        for t, q in items:
                            arrive(k, c, t, q)
                    else:
                        d = abs(c - k)
                        pair = [e for e in (k - d, k + d) if 0 <= e < n]
                        if last and len(pair) == 1 or not last and all(orders[k].index(e) >= i for e in pair):
                            for t, q in items if i > 1 or part else ():
                                for e in pair:
                                    arrive(k, e, t, q)
                        if last and part == 1:
                            for side in sides(k):
                                if near_end(k, side):
                                    forward(k, 1, 0, side).start()
            if part is None:
                work(b, 0, rows)
            else:
                work(b, begin[part], length[part])
            if last and part == 1:
                for k in range(n):
                    for side in sides(k):
                        if near_end(k, side):
                            @pl.when(z == k)
                            def _():
                                forward(k, 1, 1, side).start()
            if i:
                for k in (0, n - 1):
                    @pl.when((z == k) & (p > 0))
                    def _():
                        for q in (0, 1) if part is None else (part,):
                            running(k, orders[k][i], q, 0 if k else 1).start()

    def tell(de, dz):
        ey, ez = peer(de, dz)
        return pltpu.make_async_remote_copy(
            src_ref=sbuf.at[pl.ds(pl.multiple_of(ez * rows + de * cap, 16), cap)],
            dst_ref=srecv.at[z, pl.ds(pl.multiple_of(y * cap, 16), cap)],
            send_sem=s_send.at[de, dz], recv_sem=s_recv.at[de, dz],
            device_id=(p, ey, ez), device_id_type=MESH,
        )

    for de, dz in others:
        tell(de, dz).start()
    srecv[z, pl.ds(pl.multiple_of(y * cap, 16), cap)] = sbuf[
        pl.ds(pl.multiple_of(z * rows, 16), cap)
    ]

    for m, ref in enumerate((act, pg, pu)):
        turned[m] = ref[...].T

    def weights(j, c):
        cols = pl.ds(pl.multiple_of(j * step, step), step)
        yt, xt = yb[:, cols], xb[:, cols]
        gd_ref[:, cols] = jnp.dot(turned[0], yt, preferred_element_type=jnp.float32).astype(jnp.bfloat16)
        gg_ref[:, cols] = jnp.dot(turned[1], xt, preferred_element_type=jnp.float32).astype(jnp.bfloat16)
        gu_ref[:, cols] = jnp.dot(turned[2], xt, preferred_element_type=jnp.float32).astype(jnp.bfloat16)
        return c

    lax.fori_loop(0, width // step, weights, 0)
    for copy in writes:
        copy.start()

    def add(b, slots, q):
        def some(j, c):
            here = pl.ds(pl.multiple_of(b * rows + begin[q] + j * 16, 16), 16)
            total = dxb[here].astype(jnp.float32)
            for slot in slots:
                there = pl.ds(pl.multiple_of(slot * rows + begin[q] + j * 16, 16), 16)
                total = total + dxr[there].astype(jnp.float32)
            dxb[here] = total.astype(jnp.bfloat16)
            return c

        lax.fori_loop(0, length[q] // 16, some, 0)

    def hand(de):
        return pltpu.make_async_remote_copy(
            src_ref=dxb.at[pl.ds(pl.multiple_of(z * rows + de * cap, 16), cap)],
            dst_ref=hrecv.at[pl.ds(pl.multiple_of(y * cap, 16), cap)],
            send_sem=h_send.at[de], recv_sem=h_recv.at[y],
            device_id=(p - 1, lax.rem(y + de, experts), z), device_id_type=MESH,
        )

    for k in range(n):
        @pl.when((z == k) & (p > 0))
        def _():
            for b in finish_order(k, n):
                for q in (0, 1):
                    taken(b, q)
                    add(b, [b], q)
                    running(k, b, q, 1 if b > k else 0).start()
            slots = ([k] if k > 0 else []) + ([n] if k < n - 1 else [])
            for q in (0, 1):
                for slot in slots:
                    taken(slot, q)
                add(k, slots, q)
                for de in (range(1, experts) if q else (0,)):
                    hand(de).start()

    for de, dz in others:
        tell(de, dz).wait_recv()
    total = srecv[0]
    for k in range(1, n):
        total = total + srecv[k]
    s_ref[...] = total

    @pl.when(p < pipes - 1)
    def _():
        for e in range(experts):
            pltpu.make_async_copy(hrecv.at[pl.ds(e * cap, cap)], hrecv.at[pl.ds(e * cap, cap)], h_recv.at[e]).wait()

    @pl.when(p == pipes - 1)
    def _():
        hrecv[...] = jnp.zeros_like(hrecv)

    for copy in writes:
        copy.wait()
    for t, buffer in ((0, xb), (1, yb)):
        for de in range(1, experts):
            exchange(t, buffer, de).wait_send()
    for de, dz in others:
        tell(de, dz).wait_send()
    for k in range(n):
        @pl.when(z == k)
        def _():
            for b in range(n):
                for side in sides(k):
                    if b == k or (b < k and side) or (b > k and not side):
                        for t, q in both:
                            forward(b, t, q, side).wait_send()

        @pl.when((z == k) & (p > 0))
        def _():
            for b in range(n):
                if b != k:
                    for q in (0, 1):
                        running(k, b, q, 1 if b > k else 0).wait_send()

    @pl.when(p > 0)
    def _():
        for de in range(experts):
            hand(de).wait_send()


def tables(route_col, experts, capacity, padded):
    expert_ids = jnp.arange(experts, dtype=jnp.int32)
    onehot = (route_col[:, None] == expert_ids).astype(jnp.int32)
    earlier = jnp.cumsum(onehot, axis=0) - onehot
    slot = jnp.sum(onehot * earlier, axis=1)
    position = route_col * padded + slot
    return (jnp.arange(experts * padded, dtype=jnp.int32)[:, None] == position[None, :])


def per_device(inputs, routes, router_scores, cotangent, w_gate, w_up, w_down):
    experts, n, pipes = lax.axis_size("expert"), lax.axis_size("dp"), lax.axis_size("pipe")
    tokens, width = inputs.shape[1:]
    depth = w_gate.shape[2]
    capacity = max(2, tokens * 5 // (4 * experts))
    cap = -(-capacity // 16) * 16
    rows = experts * cap
    route_col = routes[0, :, 0]
    behind = lax.ppermute(route_col, "pipe", [(i + 1, i) for i in range(pipes - 1)])
    table = tables(route_col, experts, capacity, cap)
    following = tables(behind, experts, capacity, cap).astype(jnp.bfloat16)
    raised = jnp.exp(router_scores[0])
    weights = raised / jnp.sum(raised, axis=1, keepdims=True)
    gate = lax.optimization_barrier(weights[:, 0:1].astype(jnp.bfloat16)).astype(jnp.float32)

    vmem, hbm = pl.BlockSpec(memory_space=pltpu.VMEM), pl.BlockSpec(memory_space=pl.ANY)
    half, full = jnp.bfloat16, jnp.float32
    dma = pltpu.SemaphoreType.DMA
    grad = jax.ShapeDtypeStruct((depth, width), half)
    returned, grad_gate, grad_up, grad_down, sums = pl.pallas_call(
        functools.partial(kernel, (pipes, experts, n, cap, depth)),
        out_shape=(
            jax.ShapeDtypeStruct((rows, width), half), grad, grad, grad,
            jax.ShapeDtypeStruct((rows, 128), full),
        ),
        in_specs=[vmem] * 4 + [hbm] * 3,
        out_specs=(vmem, hbm, hbm, hbm, vmem),
        scratch_shapes=[
            *[pltpu.VMEM((depth, width), half)] * 6,
            dma((3,)), dma((3,)),
            pltpu.VMEM((2, rows, width), half),
            pltpu.VMEM((n * rows, width), half),
            pltpu.VMEM((n * rows, width), half),
            pltpu.VMEM((n * rows, width), half),
            pltpu.VMEM(((n + 1) * rows, width), half),
            pltpu.VMEM((n * rows, depth), half),
            pltpu.VMEM((n * rows, depth), half),
            pltpu.VMEM((n * rows, depth), half),
            pltpu.VMEM((3, depth, n * rows), half),
            pltpu.VMEM((n * rows, 128), full),
            pltpu.VMEM((n, rows, 128), full),
            dma((2, experts)), dma((2, experts)),
            dma((2, n, 2, 2)), dma((2, n, 2, 2)),
            dma((n, 2)), dma((n + 1, 2)),
            dma((experts, n)), dma((experts, n)),
            dma((experts,)), dma((experts,)),
        ],
        compiler_params=pltpu.CompilerParams(
            collective_id=0, has_side_effects=True, vmem_limit_bytes=62 * 1024 * 1024
        ),
    )(
        inputs[0], cotangent[0], gate, table.astype(half),
        w_gate[0, 0], w_up[0, 0], w_down[0, 0],
    )
    handed = lax.dot_general(following, returned, TN, preferred_element_type=full).astype(half)
    gate_grad = jnp.sum(jnp.where(table, sums[:, 0:1], 0.0), axis=0)[:, None] / gate
    is_first = (jnp.arange(router_scores.shape[2]) == 0).astype(full)
    score_grad = gate_grad * weights[:, 0:1] * (is_first - weights)
    return (
        score_grad[None],
        handed[None],
        grad_gate[None, None],
        grad_up[None, None],
        grad_down[None, None],
    )


def solution(mesh):
    rows = P("pipe", ("expert", "dp"), None)
    mats = P("pipe", "expert", "dp", None)
    return jax.shard_map(
        per_device, mesh=mesh, in_specs=(rows,) * 4 + (mats,) * 3,
        out_specs=(rows, rows, mats, mats, mats), check_vma=False,
    )
```
